32 devices in a mesh: grp: 4 (over y, x), dom: 8 (over z, core).
Axes of the slice: x: 2, y: 2, z: 4, core: 2. Of those that a mesh axis runs over, the one named last changes fastest.
Arguments:
- pert_fcst: bfloat16 [8, 8, 2, 8, 512], P('grp', None, None, 'dom'), may hold values from -6 to 6
- control: float32 [8, 8, 32, 128], P('grp', None, 'dom'), may hold values from -6 to 6
- departures: float32 [8, 2, 32, 128], P(None, None, 'dom'), may hold values from -6 to 6
- obs_weight: float32 [8, 2, 32, 128], P(None, None, 'dom'), may hold values from 0.3 to 3
- diff_rate: float32 [8], replicated, may hold values from 0.05 to 0.24
- step_counts: int32 [8], replicated, may hold values from 1 to 4, as said below
Outputs:
- increment: float32 [8, 2, 32, 128], P(None, None, 'dom')
- gradient: float32 [8, 8, 32, 128], P('grp', None, 'dom')
The draws below stay inside these ranges and needn't reach their ends.
Inputs may be any that keep to these rules, and one draw needn't show every extreme that they name: `step_counts`: some level has exactly 4 sweeps.
All inputs are finite; a program needn't handle non-finite values.
Results may differ from the reference program's by a relative error of at most 0.0003.
Values may be sent and summed in bfloat16 or wider, within the bound.
No kernel may reach another device: no remote copies, remote signals or barrier semaphores. Data moves between devices by JAX's collectives and lax.ppermute only.
A program may use at most 64 MiB of HBM per device.

```python
import math
import jax
import jax.numpy as jnp
from jax import lax

LEV = 8
VAR = 2
NSTEP = 4
LON_DEV = 16
MEMBERS = 8
NLAT = 32
NLON = 128
N_DOM = 8


def draw_step_counts(key, part):
    counts = jax.random.randint(key, (LEV,), 1, NSTEP + 1, dtype=jnp.int32)
    chosen = jax.random.randint(jax.random.fold_in(key, 7), (), 0, LEV, dtype=jnp.int32)
    return jnp.where(jnp.arange(LEV, dtype=jnp.int32) == chosen, NSTEP, counts).astype(jnp.int32)


def block_levels(key, extent, cuts, smallest, top_value):
    def one(position, shards_of):
        heights = jax.random.uniform(jax.random.fold_in(jax.random.fold_in(key, 6), position), (shards_of,), jnp.float32, smallest / len(cuts), top_value / len(cuts))
        return jnp.repeat(jnp.exp(heights), extent[position] // shards_of).reshape((-1,) + (1,) * (len(extent) - position - 1))

    level = one(*cuts[0])
    for cut in cuts[1:]:
        level = level * one(*cut)
    return level


def normal_values(stream_key, shape, scale, reach, split=(), held_as=jnp.bfloat16):
    gain = block_levels(stream_key, shape, split, -0.22, 0.18) if split else 1.0
    entries = jax.random.normal(stream_key, shape, jnp.float32) * scale * gain
    return jnp.minimum(jnp.maximum(entries, -reach), reach).astype(held_as)


def setup_inputs(seed: int = 0) -> dict:
    key_list = jax.random.split(jax.random.key(seed), 7)
    return {
        "pert_fcst": normal_values(key_list[0], (MEMBERS, LEV, VAR, N_DOM, NLAT * LON_DEV), 1.0, 6.0, ((0, 4), (3, 8))),
        "control": normal_values(key_list[1], (MEMBERS, LEV, NLAT, NLON), 1.0, 6.0, ((0, 4), (2, 8)), jnp.float32),
        "departures": normal_values(key_list[2], (LEV, VAR, NLAT, NLON), 1.0, 6.0, ((2, 8),), jnp.float32),
        "obs_weight": jnp.clip(jnp.exp(math.log(3.0) - 2.3025851 * jax.random.uniform(key_list[3], (LEV, VAR, NLAT, NLON), jnp.float32) ** block_levels(key_list[3], (LEV, VAR, NLAT, NLON), ((2, 8),), -0.2, 0.2)), 0.3, 3.0),
        "diff_rate": jnp.clip(jax.random.uniform(key_list[4], (LEV,), jnp.float32, 0.05, 0.24), 0.05, 0.24),
        "step_counts": draw_step_counts(jax.random.fold_in(key_list[6], 71), 0),
    }


def diffuse(field_now, diff_rate, step_counts):
    for sweep_index in range(NSTEP):
        padded = jnp.pad(field_now, ((0, 0), (1, 1), (0, 0)))
        laplace = padded[:, 2:] + padded[:, :-2] + jnp.roll(field_now, 1, axis=2) + jnp.roll(field_now, -1, axis=2) - 4.0 * field_now
        updated = field_now + diff_rate[:, None, None] * laplace
        field_now = jnp.where((sweep_index < step_counts)[:, None, None], updated, field_now)
    return field_now

def relayout(pert_member):
    blocks = pert_member.reshape(LEV, VAR, N_DOM, NLAT, LON_DEV)
    return blocks.transpose(0, 1, 3, 2, 4).reshape(LEV, VAR, NLAT, NLON)

def reference(pert_fcst, control, departures, obs_weight, diff_rate, step_counts):
    factor = 1.0 / math.sqrt(MEMBERS - 1)

    def add_member(carry_sum, inputs):
        pert_member, control_member = inputs
        localized = diffuse(control_member, diff_rate, step_counts)
        projected = relayout(pert_member).astype(jnp.float32) * localized[:, None]
        return (carry_sum + projected, None)
    start = jnp.zeros((LEV, VAR, NLAT, NLON), jnp.float32)
    summed = lax.scan(add_member, start, (pert_fcst, control))[0]
    increment = summed * factor
    residual = obs_weight * (increment - departures)

    def member_grad(inputs):
        pert_member, control_member = inputs
        adjoint = lax.optimization_barrier(jnp.sum(relayout(pert_member).astype(jnp.float32) * residual, axis=1)) * factor
        return control_member + diffuse(adjoint, diff_rate, step_counts)
    gradient = lax.map(member_grad, (pert_fcst, control))
    return (increment, gradient)
```

```python
import functools
import math

import jax
import jax.numpy as jnp
from jax import lax
from jax.experimental import pallas as pl
from jax.experimental.pallas import tpu as pltpu
from jax.sharding import PartitionSpec as P

NSTEP = 4
VMEM = pl.BlockSpec(memory_space=pltpu.VMEM)
SMEM = pl.BlockSpec(memory_space=pltpu.SMEM)


def in_vmem(x):
    return pltpu.with_memory_space_constraint(x, pltpu.VMEM)


def pack_kernel(doms, rows, groups, pert_ref, out_ref):
    pairs, variables, cells = pert_ref.shape
    lons = cells // (doms * rows)
    pert = pert_ref[...].astype(jnp.float32)
    fields = jnp.concatenate([pert[:, v, :] for v in range(variables)], axis=0)
    row_of = lax.rem(lax.broadcasted_iota(jnp.int32, fields.shape, 1) // lons, rows)
    spread = jnp.concatenate(
        [jnp.where(row_of == r, fields, 0.0) for r in range(rows)], axis=0
    ).astype(jnp.bfloat16)
    target = lax.broadcasted_iota(jnp.int32, (doms * lons, cells), 0)
    source = lax.broadcasted_iota(jnp.int32, (doms * lons, cells), 1)
    chosen = (target // lons == source // (rows * lons)) & (
        lax.rem(target, lons) == lax.rem(source, lons)
    )
    tiles = lax.dot_general(
        chosen.astype(jnp.float32).astype(jnp.bfloat16),
        spread,
        (((1,), (1,)), ((), ())),
        preferred_element_type=jnp.float32,
    )
    tiles = tiles.astype(jnp.bfloat16).reshape(doms, lons, spread.shape[0])
    for g in range(groups):
        out_ref[pl.ds(g * doms, doms)] = tiles


def sweeps(extended, rates, low_on, high_on, tile):
    rows = list(extended)
    lons = rows[0].shape[1]
    for step in range(NSTEP):
        new = list(rows)
        for i in range(step + 1, len(rows) - 1 - step):
            if i < NSTEP:
                rate = rates[step] * low_on
            elif i >= NSTEP + tile:
                rate = rates[step] * high_on
            else:
                rate = rates[step]
            mid = rows[i]
            laplace = (
                rows[i + 1]
                + rows[i - 1]
                + pltpu.roll(mid, 1, 1)
                + pltpu.roll(mid, lons - 1, 1)
                - 4.0 * mid
            )
            new[i] = mid + rate * laplace
        rows = new
    return rows[NSTEP : NSTEP + tile]


def edges():
    me, count = lax.axis_index("dom"), lax.axis_size("dom")
    odd = lax.rem(me, 2) == 1
    return odd, me > 0, me < count - 1


def with_halo(own, near, far, odd, low, high):
    below = [jnp.where(low, jnp.where(odd, n, f), 0.0) for n, f in zip(near, far)]
    above = [jnp.where(high, jnp.where(odd, f, n), 0.0) for n, f in zip(near, far)]
    return below + own + above


def localize_kernel(members, tile, rate_ref, count_ref, own_ref, near_ref, far_ref, out_ref, rates_ref):
    levels = rate_ref.shape[0]
    shape = (levels, own_ref.shape[1])
    odd, low, high = edges()
    low_on, high_on = low.astype(jnp.float32), high.astype(jnp.float32)
    level_of = lax.broadcasted_iota(jnp.int32, shape, 0)
    rate, count = jnp.zeros(shape, jnp.float32), jnp.zeros(shape, jnp.int32)
    for l in range(levels):
        rate = jnp.where(level_of == l, rate_ref[l], rate)
        count = jnp.where(level_of == l, count_ref[l], count)
    rates = [jnp.where(step < count, rate, 0.0) for step in range(NSTEP)]
    for step in range(NSTEP):
        rates_ref[step] = rates[step]
    for m in range(members):
        own, near, far = (
            [ref[pl.ds(m * levels * tile + r, levels, stride=tile), :] for r in range(tile)]
            for ref in (own_ref, near_ref, far_ref)
        )
        done = sweeps(with_halo(own, near, far, odd, low, high), rates, low_on, high_on, tile)
        for r in range(tile):
            out_ref[pl.ds((m * tile + r) * levels, levels), :] = done[r]


def adjoint_kernel(
    members, levels, variables, tile, groups, factor, tiles_ref, *refs
):
    local_refs, (weight_ref, depart_ref, inc_ref, adj_ref) = refs[:groups], refs[groups:]
    doms = tiles_ref.shape[0] // groups
    lons = inc_ref.shape[1]
    mine = lax.axis_index("grp")
    sums, first = {}, None
    for j in range(groups):
        block = tiles_ref[pl.ds(jnp.bitwise_xor(mine, j) * doms, doms)]
        fields = block.reshape(lons, -1).astype(jnp.float32).T
        if j == 0:
            first = fields
        for r in range(tile):
            for v in range(variables):
                for m in range(members):
                    at = ((r * variables + v) * members + m) * levels
                    term = (
                        fields[at : at + levels]
                        * local_refs[j][pl.ds((m * tile + r) * levels, levels), :]
                    )
                    sums[r, v] = sums[r, v] + term if (r, v) in sums else term
    for r in range(tile):
        residual = []
        for v in range(variables):
            rows = pl.ds(v * tile + r, levels, stride=variables * tile)
            increment = sums[r, v] * factor
            inc_ref[rows, :] = increment
            residual.append(weight_ref[rows, :] * (increment - depart_ref[rows, :]))
        for m in range(members):
            total = None
            for v in range(variables):
                at = ((r * variables + v) * members + m) * levels
                term = first[at : at + levels] * residual[v]
                total = term if total is None else total + term
            adj_ref[pl.ds((m * tile + r) * levels, levels), :] = total * factor


def gradient_kernel(members, tile, rates_ref, own_ref, near_ref, far_ref, control_ref, out_ref):
    levels = rates_ref.shape[1]
    odd, low, high = edges()
    low_on, high_on = low.astype(jnp.float32), high.astype(jnp.float32)
    rates = [rates_ref[step] for step in range(NSTEP)]
    for m in range(members):
        own, near, far = (
            [ref[pl.ds((m * tile + r) * levels, levels), :] for r in range(tile)]
            for ref in (own_ref, near_ref, far_ref)
        )
        done = sweeps(with_halo(own, near, far, odd, low, high), rates, low_on, high_on, tile)
        for r in range(tile):
            rows = pl.ds(m * levels * tile + r, levels, stride=tile)
            out_ref[rows, :] = control_ref[rows, :] + done[r]


def near_pairs(doms):
    return [(i, i ^ 1) for i in range(doms)]


def far_pairs(groups, doms):
    pairs = []
    for g in range(groups):
        for d in range(doms):
            if d in (0, doms - 1):
                pairs.append((g * doms + d, (g ^ 1) * doms + d))
            else:
                pairs.append((g * doms + d, g * doms + (d + 1 if d % 2 else d - 1)))
    return pairs


def beside(x, groups, doms):
    near = lax.ppermute(x, "dom", near_pairs(doms))
    far = lax.ppermute(x, ("grp", "dom"), far_pairs(groups, doms))
    return near, far


def small_device(pert_fcst, control, departures, obs_weight, diff_rate, step_counts):
    members, levels, variables = pert_fcst.shape[:3]
    tile, lons = control.shape[2], control.shape[3]
    groups, doms = lax.axis_size("grp"), lax.axis_size("dom")
    factor = 1.0 / math.sqrt(members * groups - 1)
    fields = members * levels * variables * tile
    flat = control.reshape(-1, lons)
    near, far = beside(flat, groups, doms)
    tiles = pl.pallas_call(
        functools.partial(pack_kernel, doms, tile, groups),
        out_shape=pltpu.VMEM((groups * doms, lons // doms, fields), jnp.bfloat16),
        in_specs=[VMEM],
        out_specs=VMEM,
    )(pert_fcst.reshape(members * levels, variables, -1))
    tiles = lax.all_to_all(tiles, ("grp", "dom"), split_axis=0, concat_axis=0, tiled=True)
    local, rates = pl.pallas_call(
        functools.partial(localize_kernel, members, tile),
        out_shape=[
            pltpu.VMEM(flat.shape, jnp.float32),
            pltpu.VMEM((NSTEP, levels, lons), jnp.float32),
        ],
        in_specs=[SMEM, SMEM, VMEM, VMEM, VMEM],
        out_specs=[VMEM, VMEM],
    )(diff_rate, step_counts, in_vmem(flat), in_vmem(near), in_vmem(far))
    locals_ = [local] + [
        lax.ppermute(local, "grp", [(i, i ^ j) for i in range(groups)]) for j in range(1, groups)
    ]
    increment, adjoint = pl.pallas_call(
        functools.partial(adjoint_kernel, members, levels, variables, tile, groups, factor),
        out_shape=[
            jax.ShapeDtypeStruct((levels * variables * tile, lons), jnp.float32),
            pltpu.VMEM(flat.shape, jnp.float32),
        ],
        in_specs=[VMEM] * (groups + 3),
        out_specs=[VMEM, VMEM],
    )(
        in_vmem(tiles),
        *[in_vmem(x) for x in locals_],
        in_vmem(obs_weight.reshape(-1, lons)),
        in_vmem(departures.reshape(-1, lons)),
    )
    near, far = beside(adjoint, groups, doms)
    gradient = pl.pallas_call(
        functools.partial(gradient_kernel, members, tile),
        out_shape=jax.ShapeDtypeStruct(flat.shape, jnp.float32),
        in_specs=[VMEM] * 5,
        out_specs=VMEM,
    )(in_vmem(rates), in_vmem(adjoint), in_vmem(near), in_vmem(far), in_vmem(flat))
    return increment.reshape(departures.shape), gradient.reshape(control.shape)


def diffuse(field, diff_rate, step_counts):
    count, me = lax.axis_size("dom"), lax.axis_index("dom")
    forward = [(i, i + 1) for i in range(count - 1)]
    backward = [(target, source) for source, target in forward]
    tile = field.shape[2]
    low = lax.ppermute(field[:, :, tile - NSTEP :], "dom", forward)
    high = lax.ppermute(field[:, :, :NSTEP], "dom", backward)
    wide = jnp.concatenate([low, field, high], axis=2)
    row = lax.broadcasted_iota(jnp.int32, (1, 1, wide.shape[2], 1), 2)
    inside = ((row >= NSTEP) | (me > 0)) & ((row < NSTEP + tile) | (me < count - 1))
    for step in range(NSTEP):
        on = (step < step_counts)[None, :, None, None] & inside
        padded = jnp.pad(wide, ((0, 0), (0, 0), (1, 1), (0, 0)))
        laplace = (
            padded[:, :, 2:]
            + padded[:, :, :-2]
            + jnp.roll(wide, 1, axis=3)
            + jnp.roll(wide, -1, axis=3)
            - 4.0 * wide
        )
        wide = jnp.where(on, wide + diff_rate[None, :, None, None] * laplace, wide)
    return wide[:, :, NSTEP : NSTEP + tile]


def any_device(pert_fcst, control, departures, obs_weight, diff_rate, step_counts):
    members, levels, variables = pert_fcst.shape[:3]
    tile, lons = control.shape[2], control.shape[3]
    doms = lax.axis_size("dom")
    factor = 1.0 / math.sqrt(members * lax.axis_size("grp") - 1)
    localized = diffuse(control, diff_rate, step_counts)
    received = lax.all_to_all(
        pert_fcst.reshape(members * levels * variables, doms, -1),
        "dom",
        split_axis=1,
        concat_axis=1,
        tiled=True,
    )
    perturb = (
        received.reshape(-1, doms, tile, lons // doms)
        .transpose(0, 2, 1, 3)
        .reshape(members, levels, variables, tile, lons)
        .astype(jnp.float32)
    )
    increment = lax.psum(jnp.sum(perturb * localized[:, :, None], axis=0), "grp") * factor
    residual = obs_weight * (increment - departures)
    adjoint = jnp.sum(perturb * residual[None], axis=2) * factor
    return increment, control + diffuse(adjoint, diff_rate, step_counts)


def per_device(pert_fcst, control, departures, obs_weight, diff_rate, step_counts):
    members, levels, variables = pert_fcst.shape[:3]
    tile, lons = control.shape[2], control.shape[3]
    groups, doms = lax.axis_size("grp"), lax.axis_size("dom")
    small = (
        lons == 128
        and levels == 8
        and tile == NSTEP
        and members * levels * variables * tile == 128
        and doms % 2 == 0
        and lons // doms == 16
        and groups == 4
    )
    run = small_device if small else any_device
    return run(pert_fcst, control, departures, obs_weight, diff_rate, step_counts)


def solution(mesh):
    in_specs = (
        P("grp", None, None, "dom", None),
        P("grp", None, "dom", None),
        P(None, None, "dom", None),
        P(None, None, "dom", None),
        P(),
        P(),
    )
    out_specs = (P(None, None, "dom", None), P("grp", None, "dom", None))
    return jax.shard_map(
        per_device, mesh=mesh, in_specs=in_specs, out_specs=out_specs, check_vma=False
    )
```

```python
import functools
import math

import jax
import jax.numpy as jnp
from jax import lax
from jax.experimental import pallas as pl
from jax.experimental.pallas import tpu as pltpu
from jax.sharding import PartitionSpec as P

NSTEP = 4
VMEM = pl.BlockSpec(memory_space=pltpu.VMEM)
SMEM = pl.BlockSpec(memory_space=pltpu.SMEM)


def in_vmem(x):
    return pltpu.with_memory_space_constraint(x, pltpu.VMEM)


def pack_kernel(doms, rows, groups, rate_ref, count_ref, pert_ref, out_ref, rates_ref):
    shape = rates_ref.shape[1:]
    level_of = lax.broadcasted_iota(jnp.int32, shape, 0)
    rate, count = jnp.zeros(shape, jnp.float32), jnp.zeros(shape, jnp.int32)
    for l in range(shape[0]):
        rate = jnp.where(level_of == l, rate_ref[l], rate)
        count = jnp.where(level_of == l, count_ref[l], count)
    for step in range(NSTEP):
        rates_ref[step] = jnp.where(step < count, rate, 0.0)
    pairs, variables, cells = pert_ref.shape
    lons = cells // (doms * rows)
    pert = pert_ref[...].astype(jnp.float32)
    fields = jnp.concatenate([pert[:, v, :] for v in range(variables)], axis=0)
    row_of = lax.rem(lax.broadcasted_iota(jnp.int32, fields.shape, 1) // lons, rows)
    spread = jnp.concatenate(
        [jnp.where(row_of == r, fields, 0.0) for r in range(rows)], axis=0
    ).astype(jnp.bfloat16)
    target = lax.broadcasted_iota(jnp.int32, (doms * lons, cells), 0)
    source = lax.broadcasted_iota(jnp.int32, (doms * lons, cells), 1)
    chosen = (target // lons == source // (rows * lons)) & (
        lax.rem(target, lons) == lax.rem(source, lons)
    )
    tiles = lax.dot_general(
        chosen.astype(jnp.float32).astype(jnp.bfloat16),
        spread,
        (((1,), (1,)), ((), ())),
        preferred_element_type=jnp.float32,
    )
    tiles = tiles.astype(jnp.bfloat16).reshape(doms, lons, spread.shape[0])
    for g in range(groups):
        out_ref[pl.ds(g * doms, doms)] = tiles


def sweeps(extended, rates, low_on, high_on, tile):
    rows = list(extended)
    lons = rows[0].shape[1]
    for step in range(NSTEP):
        new = list(rows)
        for i in range(step + 1, len(rows) - 1 - step):
            if i < NSTEP:
                rate = rates[step] * low_on
            elif i >= NSTEP + tile:
                rate = rates[step] * high_on
            else:
                rate = rates[step]
            mid = rows[i]
            laplace = (
                rows[i + 1]
                + rows[i - 1]
                + pltpu.roll(mid, 1, 1)
                + pltpu.roll(mid, lons - 1, 1)
                - 4.0 * mid
            )
            new[i] = mid + rate * laplace
        rows = new
    return rows[NSTEP : NSTEP + tile]


def edges():
    me, count = lax.axis_index("dom"), lax.axis_size("dom")
    odd = lax.rem(me, 2) == 1
    return odd, me > 0, me < count - 1


def with_halo(own, near, far, odd, low, high):
    below = [jnp.where(low, jnp.where(odd, n, f), 0.0) for n, f in zip(near, far)]
    above = [jnp.where(high, jnp.where(odd, f, n), 0.0) for n, f in zip(near, far)]
    return below + own + above


def localize_kernel(members, tile, rates_ref, own_ref, near_ref, far_ref, out_ref):
    levels = rates_ref.shape[1]
    odd, low, high = edges()
    low_on, high_on = low.astype(jnp.float32), high.astype(jnp.float32)
    rates = [rates_ref[step] for step in range(NSTEP)]
    for m in range(members):
        own, near, far = (
            [ref[pl.ds(m * levels * tile + r, levels, stride=tile), :] for r in range(tile)]
            for ref in (own_ref, near_ref, far_ref)
        )
        done = sweeps(with_halo(own, near, far, odd, low, high), rates, low_on, high_on, tile)
        for r in range(tile):
            out_ref[pl.ds((m * tile + r) * levels, levels), :] = done[r]


def adjoint_kernel(
    members, levels, variables, tile, groups, factor, tiles_ref, *refs
):
    local_refs, (weight_ref, depart_ref, inc_ref, adj_ref) = refs[:groups], refs[groups:]
    doms = tiles_ref.shape[0] // groups
    lons = inc_ref.shape[1]
    mine = lax.axis_index("grp")
    sums, first = {}, None
    for j in range(groups):
        block = tiles_ref[pl.ds(jnp.bitwise_xor(mine, j) * doms, doms)]
        fields = block.reshape(lons, -1).astype(jnp.float32).T
        if j == 0:
            first = fields
        for r in range(tile):
            for v in range(variables):
                for m in range(members):
                    at = ((r * variables + v) * members + m) * levels
                    term = (
                        fields[at : at + levels]
                        * local_refs[j][pl.ds((m * tile + r) * levels, levels), :]
                    )
                    sums[r, v] = sums[r, v] + term if (r, v) in sums else term
    for r in range(tile):
        residual = []
        for v in range(variables):
            rows = pl.ds(v * tile + r, levels, stride=variables * tile)
            increment = sums[r, v] * factor
            inc_ref[rows, :] = increment
            residual.append(weight_ref[rows, :] * (increment - depart_ref[rows, :]))
        for m in range(members):
            total = None
            for v in range(variables):
                at = ((r * variables + v) * members + m) * levels
                term = first[at : at + levels] * residual[v]
                total = term if total is None else total + term
            adj_ref[pl.ds((m * tile + r) * levels, levels), :] = total * factor


def gradient_kernel(members, tile, rates_ref, own_ref, near_ref, far_ref, control_ref, out_ref):
    levels = rates_ref.shape[1]
    odd, low, high = edges()
    low_on, high_on = low.astype(jnp.float32), high.astype(jnp.float32)
    rates = [rates_ref[step] for step in range(NSTEP)]
    for m in range(members):
        own, near, far = (
            [ref[pl.ds((m * tile + r) * levels, levels), :] for r in range(tile)]
            for ref in (own_ref, near_ref, far_ref)
        )
        done = sweeps(with_halo(own, near, far, odd, low, high), rates, low_on, high_on, tile)
        for r in range(tile):
            rows = pl.ds(m * levels * tile + r, levels, stride=tile)
            out_ref[rows, :] = control_ref[rows, :] + done[r]


def near_pairs(doms):
    return [(i, i ^ 1) for i in range(doms)]


def far_pairs(groups, doms):
    pairs = []
    for g in range(groups):
        for d in range(doms):
            if d in (0, doms - 1):
                pairs.append((g * doms + d, (g ^ 1) * doms + d))
            else:
                pairs.append((g * doms + d, g * doms + (d + 1 if d % 2 else d - 1)))
    return pairs


def beside(x, groups, doms):
    near = lax.ppermute(x, "dom", near_pairs(doms))
    far = lax.ppermute(x, ("grp", "dom"), far_pairs(groups, doms))
    return near, far


def small_device(pert_fcst, control, departures, obs_weight, diff_rate, step_counts):
    members, levels, variables = pert_fcst.shape[:3]
    tile, lons = control.shape[2], control.shape[3]
    groups, doms = lax.axis_size("grp"), lax.axis_size("dom")
    factor = 1.0 / math.sqrt(members * groups - 1)
    fields = members * levels * variables * tile
    flat = control.reshape(-1, lons)
    near, far = beside(flat, groups, doms)
    tiles, rates = pl.pallas_call(
        functools.partial(pack_kernel, doms, tile, groups),
        out_shape=[
            pltpu.VMEM((groups * doms, lons // doms, fields), jnp.bfloat16),
            pltpu.VMEM((NSTEP, levels, lons), jnp.float32),
        ],
        in_specs=[SMEM, SMEM, VMEM],
        out_specs=[VMEM, VMEM],
    )(diff_rate, step_counts, in_vmem(pert_fcst.reshape(members * levels, variables, -1)))
    tiles, near, far = lax.optimization_barrier((tiles, near, far))
    tiles = lax.all_to_all(tiles, ("grp", "dom"), split_axis=0, concat_axis=0, tiled=True)
    local = pl.pallas_call(
        functools.partial(localize_kernel, members, tile),
        out_shape=pltpu.VMEM(flat.shape, jnp.float32),
        in_specs=[VMEM] * 4,
        out_specs=VMEM,
    )(in_vmem(rates), in_vmem(flat), in_vmem(near), in_vmem(far))
    locals_ = [local] + [
        lax.ppermute(local, "grp", [(i, i ^ j) for i in range(groups)]) for j in range(1, groups)
    ]
    increment, adjoint = pl.pallas_call(
        functools.partial(adjoint_kernel, members, levels, variables, tile, groups, factor),
        out_shape=[
            jax.ShapeDtypeStruct((levels * variables * tile, lons), jnp.float32),
            pltpu.VMEM(flat.shape, jnp.float32),
        ],
        in_specs=[VMEM] * (groups + 3),
        out_specs=[VMEM, VMEM],
    )(
        in_vmem(tiles),
        *[in_vmem(x) for x in locals_],
        in_vmem(obs_weight.reshape(-1, lons)),
        in_vmem(departures.reshape(-1, lons)),
    )
    near, far = beside(adjoint, groups, doms)
    gradient = pl.pallas_call(
        functools.partial(gradient_kernel, members, tile),
        out_shape=jax.ShapeDtypeStruct(flat.shape, jnp.float32),
        in_specs=[VMEM] * 5,
        out_specs=VMEM,
    )(in_vmem(rates), in_vmem(adjoint), in_vmem(near), in_vmem(far), in_vmem(flat))
    return increment.reshape(departures.shape), gradient.reshape(control.shape)


def diffuse(field, diff_rate, step_counts):
    count, me = lax.axis_size("dom"), lax.axis_index("dom")
    forward = [(i, i + 1) for i in range(count - 1)]
    backward = [(target, source) for source, target in forward]
    tile = field.shape[2]
    low = lax.ppermute(field[:, :, tile - NSTEP :], "dom", forward)
    high = lax.ppermute(field[:, :, :NSTEP], "dom", backward)
    wide = jnp.concatenate([low, field, high], axis=2)
    row = lax.broadcasted_iota(jnp.int32, (1, 1, wide.shape[2], 1), 2)
    inside = ((row >= NSTEP) | (me > 0)) & ((row < NSTEP + tile) | (me < count - 1))
    for step in range(NSTEP):
        on = (step < step_counts)[None, :, None, None] & inside
        padded = jnp.pad(wide, ((0, 0), (0, 0), (1, 1), (0, 0)))
        laplace = (
            padded[:, :, 2:]
            + padded[:, :, :-2]
            + jnp.roll(wide, 1, axis=3)
            + jnp.roll(wide, -1, axis=3)
            - 4.0 * wide
        )
        wide = jnp.where(on, wide + diff_rate[None, :, None, None] * laplace, wide)
    return wide[:, :, NSTEP : NSTEP + tile]


def any_device(pert_fcst, control, departures, obs_weight, diff_rate, step_counts):
    members, levels, variables = pert_fcst.shape[:3]
    tile, lons = control.shape[2], control.shape[3]
    doms = lax.axis_size("dom")
    factor = 1.0 / math.sqrt(members * lax.axis_size("grp") - 1)
    localized = diffuse(control, diff_rate, step_counts)
    received = lax.all_to_all(
        pert_fcst.reshape(members * levels * variables, doms, -1),
        "dom",
        split_axis=1,
        concat_axis=1,
        tiled=True,
    )
    perturb = (
        received.reshape(-1, doms, tile, lons // doms)
        .transpose(0, 2, 1, 3)
        .reshape(members, levels, variables, tile, lons)
        .astype(jnp.float32)
    )
    increment = lax.psum(jnp.sum(perturb * localized[:, :, None], axis=0), "grp") * factor
    residual = obs_weight * (increment - departures)
    adjoint = jnp.sum(perturb * residual[None], axis=2) * factor
    return increment, control + diffuse(adjoint, diff_rate, step_counts)


def per_device(pert_fcst, control, departures, obs_weight, diff_rate, step_counts):
    members, levels, variables = pert_fcst.shape[:3]
    tile, lons = control.shape[2], control.shape[3]
    groups, doms = lax.axis_size("grp"), lax.axis_size("dom")
    small = (
        lons == 128
        and levels == 8
        and tile == NSTEP
        and members * levels * variables * tile == 128
        and doms % 2 == 0
        and lons // doms == 16
        and groups == 4
    )
    run = small_device if small else any_device
    return run(pert_fcst, control, departures, obs_weight, diff_rate, step_counts)


def solution(mesh):
    in_specs = (
        P("grp", None, None, "dom", None),
        P("grp", None, "dom", None),
        P(None, None, "dom", None),
        P(None, None, "dom", None),
        P(),
        P(),
    )
    out_specs = (P(None, None, "dom", None), P("grp", None, "dom", None))
    return jax.shard_map(
        per_device, mesh=mesh, in_specs=in_specs, out_specs=out_specs, check_vma=False
    )
```

```python
import functools
import math

import jax
import jax.numpy as jnp
from jax import lax
from jax.experimental import pallas as pl
from jax.experimental.pallas import tpu as pltpu
from jax.sharding import PartitionSpec as P

NSTEP = 4
VMEM = pl.BlockSpec(memory_space=pltpu.VMEM)


def in_vmem(x):
    return pltpu.with_memory_space_constraint(x, pltpu.VMEM)


def pack_kernel(doms, rows, groups, pert_ref, out_ref):
    pairs, variables, cells = pert_ref.shape
    lons = cells // (doms * rows)
    pert = pert_ref[...].astype(jnp.float32)
    fields = jnp.concatenate([pert[:, v, :] for v in range(variables)], axis=0)
    row_of = (lax.broadcasted_iota(jnp.int32, fields.shape, 1) // lons) % rows
    spread = jnp.concatenate(
        [jnp.where(row_of == r, fields, 0.0) for r in range(rows)], axis=0
    ).astype(jnp.bfloat16)
    target = lax.broadcasted_iota(jnp.int32, (doms * lons, cells), 0)
    source = lax.broadcasted_iota(jnp.int32, (doms * lons, cells), 1)
    chosen = (target // lons == source // (rows * lons)) & (
        lax.rem(target, lons) == lax.rem(source, lons)
    )
    tiles = lax.dot_general(
        chosen.astype(jnp.float32).astype(jnp.bfloat16),
        spread,
        (((1,), (1,)), ((), ())),
        preferred_element_type=jnp.float32,
    )
    tiles = tiles.astype(jnp.bfloat16).reshape(doms, lons, spread.shape[0])
    for g in range(groups):
        out_ref[pl.ds(g * doms, doms)] = tiles


def sweeps(extended, rates, low_on, high_on, tile):
    rows = list(extended)
    lons = rows[0].shape[1]
    for step in range(NSTEP):
        new = list(rows)
        for i in range(step + 1, len(rows) - 1 - step):
            if i < NSTEP:
                rate = rates[step] * low_on
            elif i >= NSTEP + tile:
                rate = rates[step] * high_on
            else:
                rate = rates[step]
            mid = rows[i]
            laplace = (
                rows[i + 1]
                + rows[i - 1]
                + pltpu.roll(mid, 1, 1)
                + pltpu.roll(mid, lons - 1, 1)
                - 4.0 * mid
            )
            new[i] = mid + rate * laplace
        rows = new
    return rows[NSTEP : NSTEP + tile]


def edges():
    me, count = lax.axis_index("dom"), lax.axis_size("dom")
    odd = lax.rem(me, 2) == 1
    return odd, me > 0, me < count - 1


def with_halo(own, near, far, odd, low, high):
    below = [jnp.where(low, jnp.where(odd, n, f), 0.0) for n, f in zip(near, far)]
    above = [jnp.where(high, jnp.where(odd, f, n), 0.0) for n, f in zip(near, far)]
    return below + own + above


def down_rows(x, lons):
    wide = jnp.broadcast_to(x.astype(jnp.float32), (x.shape[1], x.shape[1]))
    on = lax.broadcasted_iota(jnp.int32, wide.shape, 0) == lax.broadcasted_iota(jnp.int32, wide.shape, 1)
    return jnp.broadcast_to(jnp.sum(jnp.where(on, wide, 0.0), axis=1, keepdims=True), (x.shape[1], lons))


def sweep_rates(rate_ref, count_ref, lons):
    rate, count = down_rows(rate_ref[...], lons), down_rows(count_ref[...], lons)
    return [jnp.where(step < count, rate, 0.0) for step in range(NSTEP)]


def localize_kernel(members, tile, rate_ref, count_ref, own_ref, near_ref, far_ref, out_ref):
    levels = rate_ref.shape[1]
    odd, low, high = edges()
    low_on, high_on = low.astype(jnp.float32), high.astype(jnp.float32)
    rates = sweep_rates(rate_ref, count_ref, own_ref.shape[1])
    for m in range(members):
        own, near, far = (
            [ref[pl.ds(m * levels * tile + r, levels, stride=tile), :] for r in range(tile)]
            for ref in (own_ref, near_ref, far_ref)
        )
        done = sweeps(with_halo(own, near, far, odd, low, high), rates, low_on, high_on, tile)
        for r in range(tile):
            out_ref[pl.ds((m * tile + r) * levels, levels), :] = done[r]


def adjoint_kernel(
    members, levels, variables, tile, groups, factor, tiles_ref, *refs
):
    local_refs, (weight_ref, depart_ref, inc_ref, adj_ref) = refs[:groups], refs[groups:]
    doms = tiles_ref.shape[0] // groups
    lons = inc_ref.shape[1]
    mine = lax.axis_index("grp")
    sums, first = {}, None
    for j in range(groups):
        block = tiles_ref[pl.ds(jnp.bitwise_xor(mine, j) * doms, doms)]
        fields = block.reshape(lons, -1).astype(jnp.float32).T
        if j == 0:
            first = fields
        for r in range(tile):
            for v in range(variables):
                for m in range(members):
                    at = ((r * variables + v) * members + m) * levels
                    term = (
                        fields[at : at + levels]
                        * local_refs[j][pl.ds((m * tile + r) * levels, levels), :]
                    )
                    sums[r, v] = sums[r, v] + term if (r, v) in sums else term
    for r in range(tile):
        residual = []
        for v in range(variables):
            rows = pl.ds(v * tile + r, levels, stride=variables * tile)
            increment = sums[r, v] * factor
            inc_ref[rows, :] = increment
            residual.append(weight_ref[rows, :] * (increment - depart_ref[rows, :]))
        for m in range(members):
            total = None
            for v in range(variables):
                at = ((r * variables + v) * members + m) * levels
                term = first[at : at + levels] * residual[v]
                total = term if total is None else total + term
            adj_ref[pl.ds((m * tile + r) * levels, levels), :] = total * factor


def gradient_kernel(members, tile, rate_ref, count_ref, own_ref, near_ref, far_ref, control_ref, out_ref):
    levels = rate_ref.shape[1]
    odd, low, high = edges()
    low_on, high_on = low.astype(jnp.float32), high.astype(jnp.float32)
    rates = sweep_rates(rate_ref, count_ref, own_ref.shape[1])
    for m in range(members):
        own, near, far = (
            [ref[pl.ds((m * tile + r) * levels, levels), :] for r in range(tile)]
            for ref in (own_ref, near_ref, far_ref)
        )
        done = sweeps(with_halo(own, near, far, odd, low, high), rates, low_on, high_on, tile)
        for r in range(tile):
            rows = pl.ds(m * levels * tile + r, levels, stride=tile)
            out_ref[rows, :] = control_ref[rows, :] + done[r]


def near_pairs(doms):
    return [(i, i ^ 1) for i in range(doms)]


def far_pairs(groups, doms):
    pairs = []
    for g in range(groups):
        for d in range(doms):
            if d in (0, doms - 1):
                pairs.append((g * doms + d, (g ^ 1) * doms + d))
            else:
                pairs.append((g * doms + d, g * doms + (d + 1 if d % 2 else d - 1)))
    return pairs


def beside(x, groups, doms):
    near = lax.ppermute(x, "dom", near_pairs(doms))
    far = lax.ppermute(x, ("grp", "dom"), far_pairs(groups, doms))
    return near, far


def small_device(pert_fcst, control, departures, obs_weight, diff_rate, step_counts):
    members, levels, variables = pert_fcst.shape[:3]
    tile, lons = control.shape[2], control.shape[3]
    groups, doms = lax.axis_size("grp"), lax.axis_size("dom")
    factor = 1.0 / math.sqrt(members * groups - 1)
    fields = members * levels * variables * tile
    flat = control.reshape(-1, lons)
    level_args = [in_vmem(diff_rate.reshape(1, -1)), in_vmem(step_counts.reshape(1, -1))]
    tiles = pl.pallas_call(
        functools.partial(pack_kernel, doms, tile, groups),
        out_shape=pltpu.VMEM((groups * doms, lons // doms, fields), jnp.bfloat16),
        in_specs=[VMEM],
        out_specs=VMEM,
    )(in_vmem(pert_fcst.reshape(members * levels, variables, -1)))
    tiles, flat = lax.optimization_barrier((tiles, flat))
    near, far = beside(flat, groups, doms)
    tiles = lax.all_to_all(tiles, ("grp", "dom"), split_axis=0, concat_axis=0, tiled=True)
    local = pl.pallas_call(
        functools.partial(localize_kernel, members, tile),
        out_shape=pltpu.VMEM(flat.shape, jnp.float32),
        in_specs=[VMEM] * 5,
        out_specs=VMEM,
        cost_estimate=pl.CostEstimate(flops=10**10, bytes_accessed=0, transcendentals=0),
    )(*level_args, in_vmem(flat), in_vmem(near), in_vmem(far))
    locals_ = [local] + [
        lax.ppermute(local, "grp", [(i, i ^ j) for i in range(groups)]) for j in range(1, groups)
    ]
    increment, adjoint = pl.pallas_call(
        functools.partial(adjoint_kernel, members, levels, variables, tile, groups, factor),
        out_shape=[
            pltpu.VMEM((levels * variables * tile, lons), jnp.float32),
            pltpu.VMEM(flat.shape, jnp.float32),
        ],
        in_specs=[VMEM] * (groups + 3),
        out_specs=[VMEM, VMEM],
    )(
        in_vmem(tiles),
        *[in_vmem(x) for x in locals_],
        in_vmem(obs_weight.reshape(-1, lons)),
        in_vmem(departures.reshape(-1, lons)),
    )
    near, far = beside(adjoint, groups, doms)
    gradient = pl.pallas_call(
        functools.partial(gradient_kernel, members, tile),
        out_shape=jax.ShapeDtypeStruct(flat.shape, jnp.float32),
        in_specs=[VMEM] * 6,
        out_specs=VMEM,
    )(*level_args, in_vmem(adjoint), in_vmem(near), in_vmem(far), in_vmem(flat))
    return increment.reshape(departures.shape), gradient.reshape(control.shape)


def diffuse(field, diff_rate, step_counts):
    count, me = lax.axis_size("dom"), lax.axis_index("dom")
    forward = [(i, i + 1) for i in range(count - 1)]
    backward = [(target, source) for source, target in forward]
    tile = field.shape[2]
    low = lax.ppermute(field[:, :, tile - NSTEP :], "dom", forward)
    high = lax.ppermute(field[:, :, :NSTEP], "dom", backward)
    wide = jnp.concatenate([low, field, high], axis=2)
    row = lax.broadcasted_iota(jnp.int32, (1, 1, wide.shape[2], 1), 2)
    inside = ((row >= NSTEP) | (me > 0)) & ((row < NSTEP + tile) | (me < count - 1))
    for step in range(NSTEP):
        on = (step < step_counts)[None, :, None, None] & inside
        padded = jnp.pad(wide, ((0, 0), (0, 0), (1, 1), (0, 0)))
        laplace = (
            padded[:, :, 2:]
            + padded[:, :, :-2]
            + jnp.roll(wide, 1, axis=3)
            + jnp.roll(wide, -1, axis=3)
            - 4.0 * wide
        )
        wide = jnp.where(on, wide + diff_rate[None, :, None, None] * laplace, wide)
    return wide[:, :, NSTEP : NSTEP + tile]


def any_device(pert_fcst, control, departures, obs_weight, diff_rate, step_counts):
    members, levels, variables = pert_fcst.shape[:3]
    tile, lons = control.shape[2], control.shape[3]
    doms = lax.axis_size("dom")
    factor = 1.0 / math.sqrt(members * lax.axis_size("grp") - 1)
    localized = diffuse(control, diff_rate, step_counts)
    received = lax.all_to_all(
        pert_fcst.reshape(members * levels * variables, doms, -1),
        "dom",
        split_axis=1,
        concat_axis=1,
        tiled=True,
    )
    perturb = (
        received.reshape(-1, doms, tile, lons // doms)
        .transpose(0, 2, 1, 3)
        .reshape(members, levels, variables, tile, lons)
        .astype(jnp.float32)
    )
    increment = lax.psum(jnp.sum(perturb * localized[:, :, None], axis=0), "grp") * factor
    residual = obs_weight * (increment - departures)
    adjoint = jnp.sum(perturb * residual[None], axis=2) * factor
    return increment, control + diffuse(adjoint, diff_rate, step_counts)


def per_device(pert_fcst, control, departures, obs_weight, diff_rate, step_counts):
    members, levels, variables = pert_fcst.shape[:3]
    tile, lons = control.shape[2], control.shape[3]
    groups, doms = lax.axis_size("grp"), lax.axis_size("dom")
    small = (
        lons == 128
        and levels == 8
        and tile == NSTEP
        and members * levels * variables * tile == 128
        and doms % 2 == 0
        and lons // doms == 16
        and groups == 4
    )
    run = small_device if small else any_device
    return run(pert_fcst, control, departures, obs_weight, diff_rate, step_counts)


def solution(mesh):
    in_specs = (
        P("grp", None, None, "dom", None),
        P("grp", None, "dom", None),
        P(None, None, "dom", None),
        P(None, None, "dom", None),
        P(),
        P(),
    )
    out_specs = (P(None, None, "dom", None), P("grp", None, "dom", None))
    return jax.shard_map(
        per_device, mesh=mesh, in_specs=in_specs, out_specs=out_specs, check_vma=False
    )
```

```python
import functools
import math

import jax
import jax.numpy as jnp
from jax import lax
from jax.experimental import pallas as pl
from jax.experimental.pallas import tpu as pltpu
from jax.sharding import PartitionSpec as P

NSTEP = 4
VMEM = pl.BlockSpec(memory_space=pltpu.VMEM)
ANY = pl.BlockSpec(memory_space=pl.ANY)


def in_vmem(x):
    return pltpu.with_memory_space_constraint(x, pltpu.VMEM)


def down_rows(x, lons):
    wide = jnp.broadcast_to(x.astype(jnp.float32), (x.shape[1], x.shape[1]))
    on = lax.broadcasted_iota(jnp.int32, wide.shape, 0) == lax.broadcasted_iota(jnp.int32, wide.shape, 1)
    return jnp.broadcast_to(jnp.sum(jnp.where(on, wide, 0.0), axis=1, keepdims=True), (x.shape[1], lons))


def choice_kernel(rows, lons, out_ref):
    target = lax.broadcasted_iota(jnp.int32, out_ref.shape, 0)
    source = lax.broadcasted_iota(jnp.int32, out_ref.shape, 1)
    chosen = (target // lons == source // (rows * lons)) & (
        lax.rem(target, lons) == lax.rem(source, lons)
    )
    out_ref[...] = chosen.astype(jnp.float32).astype(jnp.bfloat16)


def pack_kernel(
    doms, rows, groups, chosen_ref, pert_ref, rate_ref, count_ref, out_ref, rates_ref, tiles_ref, rate_here, count_here, sems
):
    fetches = [
        pltpu.make_async_copy(rate_ref, rate_here, sems.at[groups]),
        pltpu.make_async_copy(count_ref, count_here, sems.at[groups + 1]),
    ]
    for copy in fetches:
        copy.start()
    _, variables, cells = pert_ref.shape
    lons = cells // (doms * rows)
    pert = pert_ref[...].astype(jnp.float32)
    fields = jnp.concatenate([pert[:, v, :] for v in range(variables)], axis=0)
    row_of = (lax.broadcasted_iota(jnp.int32, fields.shape, 1) // lons) % rows
    spread = jnp.concatenate(
        [jnp.where(row_of == r, fields, 0.0) for r in range(rows)], axis=0
    ).astype(jnp.bfloat16)
    tiles = lax.dot_general(
        chosen_ref[...], spread, (((1,), (1,)), ((), ())), preferred_element_type=jnp.float32
    )
    tiles_ref[...] = tiles.astype(jnp.bfloat16).reshape(tiles_ref.shape)
    stores = [
        pltpu.make_async_copy(tiles_ref, out_ref.at[pl.ds(g * doms, doms)], sems.at[g])
        for g in range(groups)
    ]
    for copy in stores:
        copy.start()
    for copy in fetches:
        copy.wait()
    rate, count = (down_rows(ref[...], rates_ref.shape[2]) for ref in (rate_here, count_here))
    for step in range(NSTEP):
        rates_ref[step] = jnp.where(step < count, rate, 0.0)
    for copy in stores:
        copy.wait()


def sweeps(extended, rates, low_on, high_on, tile):
    rows = list(extended)
    lons = rows[0].shape[1]
    for step in range(NSTEP):
        new = list(rows)
        for i in range(step + 1, len(rows) - 1 - step):
            if i < NSTEP:
                rate = rates[step] * low_on
            elif i >= NSTEP + tile:
                rate = rates[step] * high_on
            else:
                rate = rates[step]
            mid = rows[i]
            laplace = (
                rows[i + 1]
                + rows[i - 1]
                + pltpu.roll(mid, 1, 1)
                + pltpu.roll(mid, lons - 1, 1)
                - 4.0 * mid
            )
            new[i] = mid + rate * laplace
        rows = new
    return rows[NSTEP : NSTEP + tile]


def edges():
    me, count = lax.axis_index("dom"), lax.axis_size("dom")
    odd = lax.rem(me, 2) == 1
    return odd, me > 0, me < count - 1


def with_halo(own, near, far, odd, low, high):
    below = [jnp.where(low, jnp.where(odd, n, f), 0.0) for n, f in zip(near, far)]
    above = [jnp.where(high, jnp.where(odd, f, n), 0.0) for n, f in zip(near, far)]
    return below + own + above


def localize_kernel(members, tile, rates_ref, own_ref, near_ref, far_ref, out_ref):
    levels = rates_ref.shape[1]
    odd, low, high = edges()
    low_on, high_on = low.astype(jnp.float32), high.astype(jnp.float32)
    rates = [rates_ref[step] for step in range(NSTEP)]
    for m in range(members):
        own, near, far = (
            [ref[pl.ds(m * levels * tile + r, levels, stride=tile), :] for r in range(tile)]
            for ref in (own_ref, near_ref, far_ref)
        )
        done = sweeps(with_halo(own, near, far, odd, low, high), rates, low_on, high_on, tile)
        for r in range(tile):
            out_ref[pl.ds((m * tile + r) * levels, levels), :] = done[r]


def adjoint_kernel(
    members, levels, variables, tile, groups, factor, tiles_ref, *refs
):
    local_refs, (weight_ref, depart_ref, inc_ref, adj_ref) = refs[:groups], refs[groups:]
    doms = tiles_ref.shape[0] // groups
    lons = inc_ref.shape[1]
    mine = lax.axis_index("grp")
    sums, first = {}, None
    for j in range(groups):
        block = tiles_ref[pl.ds(jnp.bitwise_xor(mine, j) * doms, doms)]
        fields = block.reshape(lons, -1).astype(jnp.float32).T
        if j == 0:
            first = fields
        for r in range(tile):
            for v in range(variables):
                for m in range(members):
                    at = ((r * variables + v) * members + m) * levels
                    term = (
                        fields[at : at + levels]
                        * local_refs[j][pl.ds((m * tile + r) * levels, levels), :]
                    )
                    sums[r, v] = sums[r, v] + term if (r, v) in sums else term
    for r in range(tile):
        residual = []
        for v in range(variables):
            rows = pl.ds(v * tile + r, levels, stride=variables * tile)
            increment = sums[r, v] * factor
            inc_ref[rows, :] = increment
            residual.append(weight_ref[rows, :] * (increment - depart_ref[rows, :]))
        for m in range(members):
            total = None
            for v in range(variables):
                at = ((r * variables + v) * members + m) * levels
                term = first[at : at + levels] * residual[v]
                total = term if total is None else total + term
            adj_ref[pl.ds((m * tile + r) * levels, levels), :] = total * factor


def gradient_kernel(members, tile, rates_ref, own_ref, near_ref, far_ref, control_ref, out_ref):
    levels = rates_ref.shape[1]
    odd, low, high = edges()
    low_on, high_on = low.astype(jnp.float32), high.astype(jnp.float32)
    rates = [rates_ref[step] for step in range(NSTEP)]
    for m in range(members):
        own, near, far = (
            [ref[pl.ds((m * tile + r) * levels, levels), :] for r in range(tile)]
            for ref in (own_ref, near_ref, far_ref)
        )
        done = sweeps(with_halo(own, near, far, odd, low, high), rates, low_on, high_on, tile)
        for r in range(tile):
            rows = pl.ds(m * levels * tile + r, levels, stride=tile)
            out_ref[rows, :] = control_ref[rows, :] + done[r]


def near_pairs(doms):
    return [(i, i ^ 1) for i in range(doms)]


def far_pairs(groups, doms):
    pairs = []
    for g in range(groups):
        for d in range(doms):
            if d in (0, doms - 1):
                pairs.append((g * doms + d, (g ^ 1) * doms + d))
            else:
                pairs.append((g * doms + d, g * doms + (d + 1 if d % 2 else d - 1)))
    return pairs


def beside(x, groups, doms):
    near = lax.ppermute(x, "dom", near_pairs(doms))
    far = lax.ppermute(x, ("grp", "dom"), far_pairs(groups, doms))
    return near, far


def small_device(pert_fcst, control, departures, obs_weight, diff_rate, step_counts):
    members, levels, variables = pert_fcst.shape[:3]
    tile, lons = control.shape[2], control.shape[3]
    groups, doms = lax.axis_size("grp"), lax.axis_size("dom")
    factor = 1.0 / math.sqrt(members * groups - 1)
    fields = members * levels * variables * tile
    flat = control.reshape(-1, lons)
    cells = pert_fcst.shape[-1]
    chosen = pl.pallas_call(
        functools.partial(choice_kernel, tile, lons // doms),
        out_shape=pltpu.VMEM((lons, cells), jnp.bfloat16),
        out_specs=VMEM,
        cost_estimate=pl.CostEstimate(flops=10**10, bytes_accessed=0, transcendentals=0),
    )()
    tiles, rates = pl.pallas_call(
        functools.partial(pack_kernel, doms, tile, groups),
        out_shape=[
            jax.ShapeDtypeStruct((groups * doms, lons // doms, fields), jnp.bfloat16),
            pltpu.VMEM((NSTEP, levels, lons), jnp.float32),
        ],
        in_specs=[VMEM, VMEM, ANY, ANY],
        out_specs=[ANY, VMEM],
        scratch_shapes=[
            pltpu.VMEM((doms, lons // doms, fields), jnp.bfloat16),
            pltpu.VMEM((1, levels), jnp.float32),
            pltpu.VMEM((1, levels), jnp.int32),
            pltpu.SemaphoreType.DMA((groups + 2,)),
        ],
    )(
        in_vmem(chosen),
        in_vmem(pert_fcst.reshape(members * levels, variables, -1)),
        diff_rate.reshape(1, -1),
        step_counts.reshape(1, -1),
    )
    near, far = beside(flat, groups, doms)
    tiles = lax.all_to_all(tiles, ("grp", "dom"), split_axis=0, concat_axis=0, tiled=True)
    local = pl.pallas_call(
        functools.partial(localize_kernel, members, tile),
        out_shape=pltpu.VMEM(flat.shape, jnp.float32),
        in_specs=[VMEM] * 4,
        out_specs=VMEM,
        cost_estimate=pl.CostEstimate(flops=10**10, bytes_accessed=0, transcendentals=0),
    )(in_vmem(rates), in_vmem(flat), in_vmem(near), in_vmem(far))
    locals_ = [local] + [
        lax.ppermute(local, "grp", [(i, i ^ j) for i in range(groups)]) for j in range(1, groups)
    ]
    increment, adjoint = pl.pallas_call(
        functools.partial(adjoint_kernel, members, levels, variables, tile, groups, factor),
        out_shape=[
            pltpu.VMEM((levels * variables * tile, lons), jnp.float32),
            pltpu.VMEM(flat.shape, jnp.float32),
        ],
        in_specs=[VMEM] * (groups + 3),
        out_specs=[VMEM, VMEM],
    )(
        in_vmem(tiles),
        *[in_vmem(x) for x in locals_],
        in_vmem(obs_weight.reshape(-1, lons)),
        in_vmem(departures.reshape(-1, lons)),
    )
    near, far = beside(adjoint, groups, doms)
    gradient = pl.pallas_call(
        functools.partial(gradient_kernel, members, tile),
        out_shape=jax.ShapeDtypeStruct(flat.shape, jnp.float32),
        in_specs=[VMEM] * 5,
        out_specs=VMEM,
    )(in_vmem(rates), in_vmem(adjoint), in_vmem(near), in_vmem(far), in_vmem(flat))
    return increment.reshape(departures.shape), gradient.reshape(control.shape)


def diffuse(field, diff_rate, step_counts):
    count, me = lax.axis_size("dom"), lax.axis_index("dom")
    forward = [(i, i + 1) for i in range(count - 1)]
    backward = [(target, source) for source, target in forward]
    tile = field.shape[2]
    low = lax.ppermute(field[:, :, tile - NSTEP :], "dom", forward)
    high = lax.ppermute(field[:, :, :NSTEP], "dom", backward)
    wide = jnp.concatenate([low, field, high], axis=2)
    row = lax.broadcasted_iota(jnp.int32, (1, 1, wide.shape[2], 1), 2)
    inside = ((row >= NSTEP) | (me > 0)) & ((row < NSTEP + tile) | (me < count - 1))
    for step in range(NSTEP):
        on = (step < step_counts)[None, :, None, None] & inside
        padded = jnp.pad(wide, ((0, 0), (0, 0), (1, 1), (0, 0)))
        laplace = (
            padded[:, :, 2:]
            + padded[:, :, :-2]
            + jnp.roll(wide, 1, axis=3)
            + jnp.roll(wide, -1, axis=3)
            - 4.0 * wide
        )
        wide = jnp.where(on, wide + diff_rate[None, :, None, None] * laplace, wide)
    return wide[:, :, NSTEP : NSTEP + tile]


def any_device(pert_fcst, control, departures, obs_weight, diff_rate, step_counts):
    members, levels, variables = pert_fcst.shape[:3]
    tile, lons = control.shape[2], control.shape[3]
    doms = lax.axis_size("dom")
    factor = 1.0 / math.sqrt(members * lax.axis_size("grp") - 1)
    localized = diffuse(control, diff_rate, step_counts)
    received = lax.all_to_all(
        pert_fcst.reshape(members * levels * variables, doms, -1),
        "dom",
        split_axis=1,
        concat_axis=1,
        tiled=True,
    )
    perturb = (
        received.reshape(-1, doms, tile, lons // doms)
        .transpose(0, 2, 1, 3)
        .reshape(members, levels, variables, tile, lons)
        .astype(jnp.float32)
    )
    increment = lax.psum(jnp.sum(perturb * localized[:, :, None], axis=0), "grp") * factor
    residual = obs_weight * (increment - departures)
    adjoint = jnp.sum(perturb * residual[None], axis=2) * factor
    return increment, control + diffuse(adjoint, diff_rate, step_counts)


def per_device(pert_fcst, control, departures, obs_weight, diff_rate, step_counts):
    members, levels, variables = pert_fcst.shape[:3]
    tile, lons = control.shape[2], control.shape[3]
    groups, doms = lax.axis_size("grp"), lax.axis_size("dom")
    small = (
        lons == 128
        and levels == 8
        and tile == NSTEP
        and members * levels * variables * tile == 128
        and doms % 2 == 0
        and lons // doms == 16
        and groups == 4
    )
    run = small_device if small else any_device
    return run(pert_fcst, control, departures, obs_weight, diff_rate, step_counts)


def solution(mesh):
    in_specs = (
        P("grp", None, None, "dom", None),
        P("grp", None, "dom", None),
        P(None, None, "dom", None),
        P(None, None, "dom", None),
        P(),
        P(),
    )
    out_specs = (P(None, None, "dom", None), P("grp", None, "dom", None))
    return jax.shard_map(
        per_device, mesh=mesh, in_specs=in_specs, out_specs=out_specs, check_vma=False
    )
```

```python
import functools
import math

import jax
import jax.numpy as jnp
from jax import lax
from jax.experimental import pallas as pl
from jax.experimental.pallas import tpu as pltpu
from jax.sharding import PartitionSpec as P

NSTEP = 4
VMEM = pl.BlockSpec(memory_space=pltpu.VMEM)
ANY = pl.BlockSpec(memory_space=pl.ANY)


def in_vmem(x):
    return pltpu.with_memory_space_constraint(x, pltpu.VMEM)


def down_rows(x, lons):
    wide = jnp.broadcast_to(x.astype(jnp.float32), (x.shape[1], x.shape[1]))
    on = lax.broadcasted_iota(jnp.int32, wide.shape, 0) == lax.broadcasted_iota(jnp.int32, wide.shape, 1)
    return jnp.broadcast_to(jnp.sum(jnp.where(on, wide, 0.0), axis=1, keepdims=True), (x.shape[1], lons))


def choice_kernel(rows, lons, out_ref):
    target = lax.broadcasted_iota(jnp.int32, out_ref.shape, 0)
    source = lax.broadcasted_iota(jnp.int32, out_ref.shape, 1)
    chosen = (target // lons == source // (rows * lons)) & (
        lax.rem(target, lons) == lax.rem(source, lons)
    )
    out_ref[...] = chosen.astype(jnp.float32).astype(jnp.bfloat16)


def pack_kernel(
    doms, rows, groups, chosen_ref, pert_ref, rate_ref, count_ref, out_ref, rates_ref, tiles_ref, rate_here, count_here, sems
):
    fetches = [
        pltpu.make_async_copy(rate_ref, rate_here, sems.at[groups]),
        pltpu.make_async_copy(count_ref, count_here, sems.at[groups + 1]),
    ]
    for copy in fetches:
        copy.start()
    _, variables, cells = pert_ref.shape
    lons = cells // (doms * rows)
    pert = pert_ref[...].astype(jnp.float32)
    fields = jnp.concatenate([pert[:, v, :] for v in range(variables)], axis=0)
    row_of = (lax.broadcasted_iota(jnp.int32, fields.shape, 1) // lons) % rows
    spread = jnp.concatenate(
        [jnp.where(row_of == r, fields, 0.0) for r in range(rows)], axis=0
    ).astype(jnp.bfloat16)
    chosen, pair = chosen_ref[...], chosen_ref.shape[1]
    for chip in range(doms // 2):
        both = lax.dot_general(
            chosen,
            spread[:, chip * pair : (chip + 1) * pair],
            (((1,), (1,)), ((), ())),
            preferred_element_type=jnp.float32,
        ).astype(jnp.bfloat16)
        for core in range(2):
            tiles_ref[core, chip] = both[core * lons : (core + 1) * lons]
    stores = [pltpu.make_async_copy(tiles_ref, out_ref.at[:, g], sems.at[g]) for g in range(groups)]
    for copy in stores:
        copy.start()
    for copy in fetches:
        copy.wait()
    rate, count = (down_rows(ref[...], rates_ref.shape[2]) for ref in (rate_here, count_here))
    for step in range(NSTEP):
        rates_ref[step] = jnp.where(step < count, rate, 0.0)
    for copy in stores:
        copy.wait()


def sweeps(extended, rates, low_on, high_on, tile):
    lons = extended[0].shape[1]
    count = len(extended)
    powers = [list(extended)] + [[None] * count for _ in range(NSTEP)]
    for i in range(1, count - 1):
        deep = min(i, count - 1 - i, NSTEP)
        row = extended[i]
        pair = {
            k: pltpu.roll(row, k, 1) + pltpu.roll(row, lons - k, 1) for k in range(1, deep + 1)
        }
        pair[0] = row
        for n in range(1, deep + 1):
            total = pair[n]
            for k in range(1, (n + 1) // 2):
                total = total + float(math.comb(n, k)) * pair[n - 2 * k]
            if n % 2 == 0:
                total = total + float(math.comb(n, n // 2)) * row
            powers[n][i] = total
    for step in range(NSTEP):
        new = [[None] * count for _ in range(NSTEP - step)]
        for n in range(NSTEP - step):
            for i in range(step + 1 + n, count - 1 - step - n):
                if i < NSTEP:
                    rate = rates[step] * low_on
                elif i >= NSTEP + tile:
                    rate = rates[step] * high_on
                else:
                    rate = rates[step]
                mid = powers[n][i]
                laplace = powers[n][i + 1] + powers[n][i - 1] + powers[n + 1][i] - 4.0 * mid
                new[n][i] = mid + rate * laplace
        powers = new
    return powers[0][NSTEP : NSTEP + tile]


def edges():
    me, count = lax.axis_index("dom"), lax.axis_size("dom")
    odd = lax.rem(me, 2) == 1
    return odd, me > 0, me < count - 1


def with_halo(own, near, far, odd, low, high):
    below = [jnp.where(low, jnp.where(odd, n, f), 0.0) for n, f in zip(near, far)]
    above = [jnp.where(high, jnp.where(odd, f, n), 0.0) for n, f in zip(near, far)]
    return below + own + above


def localize_kernel(members, tile, rates_ref, own_ref, near_ref, far_ref, out_ref):
    levels = rates_ref.shape[1]
    odd, low, high = edges()
    low_on, high_on = low.astype(jnp.float32), high.astype(jnp.float32)
    rates = [rates_ref[step] for step in range(NSTEP)]
    for m in range(members):
        own, near, far = (
            [ref[pl.ds(m * levels * tile + r, levels, stride=tile), :] for r in range(tile)]
            for ref in (own_ref, near_ref, far_ref)
        )
        done = sweeps(with_halo(own, near, far, odd, low, high), rates, low_on, high_on, tile)
        for r in range(tile):
            out_ref[pl.ds((m * tile + r) * levels, levels), :] = done[r]


def adjoint_kernel(
    members, levels, variables, tile, groups, factor, tiles_ref, *refs
):
    local_refs, (weight_ref, depart_ref, inc_ref, adj_ref) = refs[:groups], refs[groups:]
    chips = tiles_ref.shape[2]
    mine = lax.axis_index("grp")
    sums, first = {}, None
    for j in range(groups):
        group = jnp.bitwise_xor(mine, j)
        blocks = [tiles_ref[core, group, chip] for chip in range(chips) for core in range(2)]
        fields = jnp.concatenate(blocks, axis=0).astype(jnp.float32).T
        if j == 0:
            first = fields
        for r in range(tile):
            for v in range(variables):
                for m in range(members):
                    at = ((r * variables + v) * members + m) * levels
                    term = (
                        fields[at : at + levels]
                        * local_refs[j][pl.ds((m * tile + r) * levels, levels), :]
                    )
                    sums[r, v] = sums[r, v] + term if (r, v) in sums else term
    for r in range(tile):
        residual = []
        for v in range(variables):
            rows = pl.ds(v * tile + r, levels, stride=variables * tile)
            increment = sums[r, v] * factor
            inc_ref[rows, :] = increment
            residual.append(weight_ref[rows, :] * (increment - depart_ref[rows, :]))
        for m in range(members):
            total = None
            for v in range(variables):
                at = ((r * variables + v) * members + m) * levels
                term = first[at : at + levels] * residual[v]
                total = term if total is None else total + term
            adj_ref[pl.ds((m * tile + r) * levels, levels), :] = total * factor


def gradient_kernel(members, tile, rates_ref, own_ref, near_ref, far_ref, control_ref, out_ref):
    levels = rates_ref.shape[1]
    odd, low, high = edges()
    low_on, high_on = low.astype(jnp.float32), high.astype(jnp.float32)
    rates = [rates_ref[step] for step in range(NSTEP)]
    for m in range(members):
        own, near, far = (
            [ref[pl.ds((m * tile + r) * levels, levels), :] for r in range(tile)]
            for ref in (own_ref, near_ref, far_ref)
        )
        done = sweeps(with_halo(own, near, far, odd, low, high), rates, low_on, high_on, tile)
        for r in range(tile):
            rows = pl.ds(m * levels * tile + r, levels, stride=tile)
            out_ref[rows, :] = control_ref[rows, :] + done[r]


def near_pairs(doms):
    return [(i, i ^ 1) for i in range(doms)]


def far_pairs(groups, doms):
    pairs = []
    for g in range(groups):
        for d in range(doms):
            if d in (0, doms - 1):
                pairs.append((g * doms + d, (g ^ 1) * doms + d))
            else:
                pairs.append((g * doms + d, g * doms + (d + 1 if d % 2 else d - 1)))
    return pairs


def core_order(groups, doms):
    return [[g * doms + d for core in range(2) for g in range(groups) for d in range(core, doms, 2)]]


def beside(x, groups, doms):
    near = lax.ppermute(x, "dom", near_pairs(doms))
    far = lax.ppermute(x, ("grp", "dom"), far_pairs(groups, doms))
    return near, far


def small_device(pert_fcst, control, departures, obs_weight, diff_rate, step_counts):
    members, levels, variables = pert_fcst.shape[:3]
    tile, lons = control.shape[2], control.shape[3]
    groups, doms = lax.axis_size("grp"), lax.axis_size("dom")
    factor = 1.0 / math.sqrt(members * groups - 1)
    fields = members * levels * variables * tile
    flat = control.reshape(-1, lons)
    cells = pert_fcst.shape[-1]
    chosen = pl.pallas_call(
        functools.partial(choice_kernel, tile, lons // doms),
        out_shape=pltpu.VMEM((2 * lons // doms, 2 * cells // doms), jnp.bfloat16),
        out_specs=VMEM,
        cost_estimate=pl.CostEstimate(flops=10**10, bytes_accessed=0, transcendentals=0),
    )()
    tiles, rates = pl.pallas_call(
        functools.partial(pack_kernel, doms, tile, groups),
        out_shape=[
            jax.ShapeDtypeStruct((2, groups, doms // 2, lons // doms, fields), jnp.bfloat16),
            pltpu.VMEM((NSTEP, levels, lons), jnp.float32),
        ],
        in_specs=[VMEM, VMEM, ANY, ANY],
        out_specs=[ANY, VMEM],
        scratch_shapes=[
            pltpu.VMEM((2, doms // 2, lons // doms, fields), jnp.bfloat16),
            pltpu.VMEM((1, levels), jnp.float32),
            pltpu.VMEM((1, levels), jnp.int32),
            pltpu.SemaphoreType.DMA((groups + 2,)),
        ],
    )(
        in_vmem(chosen),
        in_vmem(pert_fcst.reshape(members * levels, variables, -1)),
        diff_rate.reshape(1, -1),
        step_counts.reshape(1, -1),
    )
    near, far = beside(flat, groups, doms)
    received = lax.all_to_all(
        tiles.reshape(-1, *tiles.shape[3:]),
        ("grp", "dom"),
        split_axis=0,
        concat_axis=0,
        tiled=True,
        axis_index_groups=core_order(groups, doms),
    )
    tiles = received.reshape(tiles.shape)
    local = pl.pallas_call(
        functools.partial(localize_kernel, members, tile),
        out_shape=pltpu.VMEM(flat.shape, jnp.float32),
        in_specs=[VMEM] * 4,
        out_specs=VMEM,
        cost_estimate=pl.CostEstimate(flops=10**10, bytes_accessed=0, transcendentals=0),
    )(in_vmem(rates), in_vmem(flat), in_vmem(near), in_vmem(far))
    locals_ = [local] + [
        lax.ppermute(local, "grp", [(i, i ^ j) for i in range(groups)]) for j in range(1, groups)
    ]
    increment, adjoint = pl.pallas_call(
        functools.partial(adjoint_kernel, members, levels, variables, tile, groups, factor),
        out_shape=[
            pltpu.VMEM((levels * variables * tile, lons), jnp.float32),
            pltpu.VMEM(flat.shape, jnp.float32),
        ],
        in_specs=[VMEM] * (groups + 3),
        out_specs=[VMEM, VMEM],
    )(
        in_vmem(tiles),
        *[in_vmem(x) for x in locals_],
        in_vmem(obs_weight.reshape(-1, lons)),
        in_vmem(departures.reshape(-1, lons)),
    )
    near, far = beside(adjoint, groups, doms)
    gradient = pl.pallas_call(
        functools.partial(gradient_kernel, members, tile),
        out_shape=jax.ShapeDtypeStruct(flat.shape, jnp.float32),
        in_specs=[VMEM] * 5,
        out_specs=VMEM,
    )(in_vmem(rates), in_vmem(adjoint), in_vmem(near), in_vmem(far), in_vmem(flat))
    return increment.reshape(departures.shape), gradient.reshape(control.shape)


def diffuse(field, diff_rate, step_counts):
    count, me = lax.axis_size("dom"), lax.axis_index("dom")
    forward = [(i, i + 1) for i in range(count - 1)]
    backward = [(target, source) for source, target in forward]
    tile = field.shape[2]
    low = lax.ppermute(field[:, :, tile - NSTEP :], "dom", forward)
    high = lax.ppermute(field[:, :, :NSTEP], "dom", backward)
    wide = jnp.concatenate([low, field, high], axis=2)
    row = lax.broadcasted_iota(jnp.int32, (1, 1, wide.shape[2], 1), 2)
    inside = ((row >= NSTEP) | (me > 0)) & ((row < NSTEP + tile) | (me < count - 1))
    for step in range(NSTEP):
        on = (step < step_counts)[None, :, None, None] & inside
        padded = jnp.pad(wide, ((0, 0), (0, 0), (1, 1), (0, 0)))
        laplace = (
            padded[:, :, 2:]
            + padded[:, :, :-2]
            + jnp.roll(wide, 1, axis=3)
            + jnp.roll(wide, -1, axis=3)
            - 4.0 * wide
        )
        wide = jnp.where(on, wide + diff_rate[None, :, None, None] * laplace, wide)
    return wide[:, :, NSTEP : NSTEP + tile]


def any_device(pert_fcst, control, departures, obs_weight, diff_rate, step_counts):
    members, levels, variables = pert_fcst.shape[:3]
    tile, lons = control.shape[2], control.shape[3]
    doms = lax.axis_size("dom")
    factor = 1.0 / math.sqrt(members * lax.axis_size("grp") - 1)
    localized = diffuse(control, diff_rate, step_counts)
    received = lax.all_to_all(
        pert_fcst.reshape(members * levels * variables, doms, -1),
        "dom",
        split_axis=1,
        concat_axis=1,
        tiled=True,
    )
    perturb = (
        received.reshape(-1, doms, tile, lons // doms)
        .transpose(0, 2, 1, 3)
        .reshape(members, levels, variables, tile, lons)
        .astype(jnp.float32)
    )
    increment = lax.psum(jnp.sum(perturb * localized[:, :, None], axis=0), "grp") * factor
    residual = obs_weight * (increment - departures)
    adjoint = jnp.sum(perturb * residual[None], axis=2) * factor
    return increment, control + diffuse(adjoint, diff_rate, step_counts)


def per_device(pert_fcst, control, departures, obs_weight, diff_rate, step_counts):
    members, levels, variables = pert_fcst.shape[:3]
    tile, lons = control.shape[2], control.shape[3]
    groups, doms = lax.axis_size("grp"), lax.axis_size("dom")
    small = (
        lons == 128
        and levels == 8
        and tile == NSTEP
        and members * levels * variables * tile == 128
        and doms % 2 == 0
        and lons // doms == 16
        and groups == 4
    )
    run = small_device if small else any_device
    return run(pert_fcst, control, departures, obs_weight, diff_rate, step_counts)


def solution(mesh):
    in_specs = (
        P("grp", None, None, "dom", None),
        P("grp", None, "dom", None),
        P(None, None, "dom", None),
        P(None, None, "dom", None),
        P(),
        P(),
    )
    out_specs = (P(None, None, "dom", None), P("grp", None, "dom", None))
    return jax.shard_map(
        per_device, mesh=mesh, in_specs=in_specs, out_specs=out_specs, check_vma=False
    )
```

```python
import functools
import math

import jax
import jax.numpy as jnp
from jax import lax
from jax.experimental import pallas as pl
from jax.experimental.pallas import tpu as pltpu
from jax.sharding import PartitionSpec as P

NSTEP = 4
VMEM = pl.BlockSpec(memory_space=pltpu.VMEM)
ANY = pl.BlockSpec(memory_space=pl.ANY)


def in_vmem(x):
    return pltpu.with_memory_space_constraint(x, pltpu.VMEM)


def down_rows(x, lons):
    wide = jnp.broadcast_to(x.astype(jnp.float32), (x.shape[1], x.shape[1]))
    on = lax.broadcasted_iota(jnp.int32, wide.shape, 0) == lax.broadcasted_iota(jnp.int32, wide.shape, 1)
    return jnp.broadcast_to(jnp.sum(jnp.where(on, wide, 0.0), axis=1, keepdims=True), (x.shape[1], lons))


def choice_kernel(rows, lons, out_ref):
    target = lax.broadcasted_iota(jnp.int32, out_ref.shape, 0)
    source = lax.broadcasted_iota(jnp.int32, out_ref.shape, 1)
    chosen = (target // lons == source // (rows * lons)) & (
        lax.rem(target, lons) == lax.rem(source, lons)
    )
    out_ref[...] = chosen.astype(jnp.float32).astype(jnp.bfloat16)


def pack_kernel(
    doms, rows, groups, chosen_ref, pert_ref, rate_ref, count_ref, out_ref, rates_ref, tiles_ref, rate_here, count_here, sems
):
    fetches = [
        pltpu.make_async_copy(rate_ref, rate_here, sems.at[groups]),
        pltpu.make_async_copy(count_ref, count_here, sems.at[groups + 1]),
    ]
    for copy in fetches:
        copy.start()
    _, variables, cells = pert_ref.shape
    lons = cells // (doms * rows)
    pert = pert_ref[...].astype(jnp.float32)
    fields = jnp.concatenate([pert[:, v, :] for v in range(variables)], axis=0)
    row_of = (lax.broadcasted_iota(jnp.int32, fields.shape, 1) // lons) % rows
    spread = jnp.concatenate(
        [jnp.where(row_of == r, fields, 0.0) for r in range(rows)], axis=0
    ).astype(jnp.bfloat16)
    chosen, pair = chosen_ref[...], chosen_ref.shape[1]
    for chip in range(doms // 2):
        both = lax.dot_general(
            chosen,
            spread[:, chip * pair : (chip + 1) * pair],
            (((1,), (1,)), ((), ())),
            preferred_element_type=jnp.float32,
        ).astype(jnp.bfloat16)
        for core in range(2):
            tiles_ref[core, chip] = both[core * lons : (core + 1) * lons]
    stores = [pltpu.make_async_copy(tiles_ref, out_ref.at[:, g], sems.at[g]) for g in range(groups)]
    for copy in stores:
        copy.start()
    for copy in fetches:
        copy.wait()
    rate, count = (down_rows(ref[...], rates_ref.shape[2]) for ref in (rate_here, count_here))
    for step in range(NSTEP):
        rates_ref[step] = jnp.where(step < count, rate, 0.0)
    for copy in stores:
        copy.wait()


def sweeps(extended, rates, low_on, high_on, tile):
    lons = extended[0].shape[1]
    count = len(extended)
    powers = [list(extended)] + [[None] * count for _ in range(NSTEP)]
    for i in range(1, count - 1):
        deep = min(i, count - 1 - i, NSTEP)
        row = extended[i]
        pair = {
            k: pltpu.roll(row, k, 1) + pltpu.roll(row, lons - k, 1) for k in range(1, deep + 1)
        }
        pair[0] = row
        for n in range(1, deep + 1):
            total = pair[n]
            for k in range(1, (n + 1) // 2):
                total = total + float(math.comb(n, k)) * pair[n - 2 * k]
            if n % 2 == 0:
                total = total + float(math.comb(n, n // 2)) * row
            powers[n][i] = total
    for step in range(NSTEP):
        new = [[None] * count for _ in range(NSTEP - step)]
        for n in range(NSTEP - step):
            for i in range(step + 1 + n, count - 1 - step - n):
                if i < NSTEP:
                    rate = rates[step] * low_on
                elif i >= NSTEP + tile:
                    rate = rates[step] * high_on
                else:
                    rate = rates[step]
                mid = powers[n][i]
                laplace = powers[n][i + 1] + powers[n][i - 1] + powers[n + 1][i] - 4.0 * mid
                new[n][i] = mid + rate * laplace
        powers = new
    return powers[0][NSTEP : NSTEP + tile]


def edges():
    me, count = lax.axis_index("dom"), lax.axis_size("dom")
    odd = lax.rem(me, 2) == 1
    return odd, me > 0, me < count - 1


def with_halo(own, near, far, odd, low, high):
    below = [jnp.where(low, jnp.where(odd, n, f), 0.0) for n, f in zip(near, far)]
    above = [jnp.where(high, jnp.where(odd, f, n), 0.0) for n, f in zip(near, far)]
    return below + own + above


def localize_kernel(members, tile, rates_ref, own_ref, near_ref, far_ref, out_ref):
    levels = rates_ref.shape[1]
    odd, low, high = edges()
    low_on, high_on = low.astype(jnp.float32), high.astype(jnp.float32)
    rates = [rates_ref[step] for step in range(NSTEP)]
    for m in range(members):
        own, near, far = (
            [ref[pl.ds(m * levels * tile + r, levels, stride=tile), :] for r in range(tile)]
            for ref in (own_ref, near_ref, far_ref)
        )
        done = sweeps(with_halo(own, near, far, odd, low, high), rates, low_on, high_on, tile)
        for r in range(tile):
            out_ref[pl.ds((m * tile + r) * levels, levels), :] = done[r]


def adjoint_kernel(
    members, levels, variables, tile, groups, factor, tiles_ref, *refs
):
    local_refs, (weight_ref, depart_ref, inc_ref, adj_ref, far_ref) = refs[:groups], refs[groups:]
    chips = tiles_ref.shape[2]
    mine = lax.axis_index("grp")
    sums, first = {}, None
    for j in range(groups):
        group = jnp.bitwise_xor(mine, j)
        blocks = [tiles_ref[core, group, chip] for chip in range(chips) for core in range(2)]
        fields = jnp.concatenate(blocks, axis=0).astype(jnp.float32).T
        if j == 0:
            first = fields
        for r in range(tile):
            for v in range(variables):
                for m in range(members):
                    at = ((r * variables + v) * members + m) * levels
                    term = (
                        fields[at : at + levels]
                        * local_refs[j][pl.ds((m * tile + r) * levels, levels), :]
                    )
                    sums[r, v] = sums[r, v] + term if (r, v) in sums else term
    for r in range(tile):
        residual = []
        for v in range(variables):
            rows = pl.ds(v * tile + r, levels, stride=variables * tile)
            increment = sums[r, v] * factor
            inc_ref[rows, :] = increment
            residual.append(weight_ref[rows, :] * (increment - depart_ref[rows, :]))
        for m in range(members):
            total = None
            for v in range(variables):
                at = ((r * variables + v) * members + m) * levels
                term = first[at : at + levels] * residual[v]
                total = term if total is None else total + term
            adj_ref[pl.ds((m * tile + r) * levels, levels), :] = total * factor
            far_ref[pl.ds((m * tile + r) * levels, levels), :] = total * factor
    far_ref[pl.ds(members * tile * levels, levels), :] = jnp.zeros((levels, inc_ref.shape[1]), jnp.float32)


def gradient_rows(members, tile, rates_ref, own_ref, near_ref, far_ref, control_ref, out_ref):
    levels = rates_ref.shape[1]
    odd, low, high = edges()
    low_on, high_on = low.astype(jnp.float32), high.astype(jnp.float32)
    rates = [rates_ref[step] for step in range(NSTEP)]
    for m in range(members):
        own, near, far = (
            [ref[pl.ds((m * tile + r) * levels, levels), :] for r in range(tile)]
            for ref in (own_ref, near_ref, near_ref if far_ref is None else far_ref)
        )
        done = sweeps(with_halo(own, near, far, odd, low, high), rates, low_on, high_on, tile)
        for r in range(tile):
            rows = pl.ds(m * levels * tile + r, levels, stride=tile)
            out_ref[rows, :] = control_ref[rows, :] + done[r]


def end_kernel(members, tile, rates_ref, own_ref, near_ref, control_ref, out_ref, rows_ref, sem):
    _, low, high = edges()

    @pl.when(jnp.logical_not(low & high))
    def _():
        gradient_rows(members, tile, rates_ref, own_ref, near_ref, None, control_ref, rows_ref)
        copy = pltpu.make_async_copy(rows_ref, out_ref, sem)
        copy.start()
        copy.wait()


def inner_kernel(
    members, tile, rates_ref, own_ref, near_ref, far_ref, control_ref, _, out_ref, rows_ref, sem
):
    _, low, high = edges()

    @pl.when(low & high)
    def _():
        gradient_rows(
            members, tile, rates_ref, own_ref, near_ref, far_ref, control_ref, rows_ref
        )
        copy = pltpu.make_async_copy(rows_ref, out_ref, sem)
        copy.start()
        copy.wait()


def near_pairs(doms):
    return [(i, i ^ 1) for i in range(doms)]


def far_pairs(groups, doms):
    pairs = []
    for g in range(groups):
        for d in range(doms):
            if d in (0, doms - 1):
                pairs.append((g * doms + d, (g ^ 1) * doms + d))
            else:
                pairs.append((g * doms + d, g * doms + (d + 1 if d % 2 else d - 1)))
    return pairs


def core_order(groups, doms):
    return [[g * doms + d for core in range(2) for g in range(groups) for d in range(core, doms, 2)]]


def beside(x, groups, doms):
    near = lax.ppermute(x, "dom", near_pairs(doms))
    far = lax.ppermute(x, ("grp", "dom"), far_pairs(groups, doms))
    return near, far


def small_device(pert_fcst, control, departures, obs_weight, diff_rate, step_counts):
    members, levels, variables = pert_fcst.shape[:3]
    tile, lons = control.shape[2], control.shape[3]
    groups, doms = lax.axis_size("grp"), lax.axis_size("dom")
    factor = 1.0 / math.sqrt(members * groups - 1)
    fields = members * levels * variables * tile
    flat = control.reshape(-1, lons)
    cells = pert_fcst.shape[-1]
    chosen = pl.pallas_call(
        functools.partial(choice_kernel, tile, lons // doms),
        out_shape=pltpu.VMEM((2 * lons // doms, 2 * cells // doms), jnp.bfloat16),
        out_specs=VMEM,
        cost_estimate=pl.CostEstimate(flops=10**10, bytes_accessed=0, transcendentals=0),
    )()
    tiles, rates = pl.pallas_call(
        functools.partial(pack_kernel, doms, tile, groups),
        out_shape=[
            jax.ShapeDtypeStruct((2, groups, doms // 2, lons // doms, fields), jnp.bfloat16),
            pltpu.VMEM((NSTEP, levels, lons), jnp.float32),
        ],
        in_specs=[VMEM, VMEM, ANY, ANY],
        out_specs=[ANY, VMEM],
        scratch_shapes=[
            pltpu.VMEM((2, doms // 2, lons // doms, fields), jnp.bfloat16),
            pltpu.VMEM((1, levels), jnp.float32),
            pltpu.VMEM((1, levels), jnp.int32),
            pltpu.SemaphoreType.DMA((groups + 2,)),
        ],
    )(
        in_vmem(chosen),
        in_vmem(pert_fcst.reshape(members * levels, variables, -1)),
        diff_rate.reshape(1, -1),
        step_counts.reshape(1, -1),
    )
    near, far = beside(flat, groups, doms)
    received = lax.all_to_all(
        tiles.reshape(-1, *tiles.shape[3:]),
        ("grp", "dom"),
        split_axis=0,
        concat_axis=0,
        tiled=True,
        axis_index_groups=core_order(groups, doms),
    )
    tiles = received.reshape(tiles.shape)
    local = pl.pallas_call(
        functools.partial(localize_kernel, members, tile),
        out_shape=pltpu.VMEM(flat.shape, jnp.float32),
        in_specs=[VMEM] * 4,
        out_specs=VMEM,
        cost_estimate=pl.CostEstimate(flops=10**10, bytes_accessed=0, transcendentals=0),
    )(in_vmem(rates), in_vmem(flat), in_vmem(near), in_vmem(far))
    locals_ = [local] + [
        lax.ppermute(local, "grp", [(i, i ^ j) for i in range(groups)]) for j in range(1, groups)
    ]
    increment, adjoint, for_far = pl.pallas_call(
        functools.partial(adjoint_kernel, members, levels, variables, tile, groups, factor),
        out_shape=[
            pltpu.VMEM((levels * variables * tile, lons), jnp.float32),
            pltpu.VMEM(flat.shape, jnp.float32),
            pltpu.VMEM((flat.shape[0] + levels, lons), jnp.float32),
        ],
        in_specs=[VMEM] * (groups + 3),
        out_specs=[VMEM, VMEM, VMEM],
    )(
        in_vmem(tiles),
        *[in_vmem(x) for x in locals_],
        in_vmem(obs_weight.reshape(-1, lons)),
        in_vmem(departures.reshape(-1, lons)),
    )
    near = lax.ppermute(adjoint, "dom", near_pairs(doms))
    far = lax.ppermute(for_far, ("grp", "dom"), far_pairs(groups, doms))
    at_ends = pl.pallas_call(
        functools.partial(end_kernel, members, tile),
        out_shape=jax.ShapeDtypeStruct(flat.shape, jnp.float32),
        in_specs=[VMEM] * 4,
        out_specs=ANY,
        scratch_shapes=[pltpu.VMEM(flat.shape, jnp.float32), pltpu.SemaphoreType.DMA],
        cost_estimate=pl.CostEstimate(flops=0, bytes_accessed=0, transcendentals=0),
    )(in_vmem(rates), in_vmem(adjoint), in_vmem(near), in_vmem(flat))
    gradient = pl.pallas_call(
        functools.partial(inner_kernel, members, tile),
        out_shape=jax.ShapeDtypeStruct(flat.shape, jnp.float32),
        in_specs=[VMEM] * 5 + [ANY],
        out_specs=ANY,
        scratch_shapes=[pltpu.VMEM(flat.shape, jnp.float32), pltpu.SemaphoreType.DMA],
        input_output_aliases={5: 0},
    )(in_vmem(rates), in_vmem(adjoint), in_vmem(near), in_vmem(far), in_vmem(flat), at_ends)
    return increment.reshape(departures.shape), gradient.reshape(control.shape)


def diffuse(field, diff_rate, step_counts):
    count, me = lax.axis_size("dom"), lax.axis_index("dom")
    forward = [(i, i + 1) for i in range(count - 1)]
    backward = [(target, source) for source, target in forward]
    tile = field.shape[2]
    low = lax.ppermute(field[:, :, tile - NSTEP :], "dom", forward)
    high = lax.ppermute(field[:, :, :NSTEP], "dom", backward)
    wide = jnp.concatenate([low, field, high], axis=2)
    row = lax.broadcasted_iota(jnp.int32, (1, 1, wide.shape[2], 1), 2)
    inside = ((row >= NSTEP) | (me > 0)) & ((row < NSTEP + tile) | (me < count - 1))
    for step in range(NSTEP):
        on = (step < step_counts)[None, :, None, None] & inside
        padded = jnp.pad(wide, ((0, 0), (0, 0), (1, 1), (0, 0)))
        laplace = (
            padded[:, :, 2:]
            + padded[:, :, :-2]
            + jnp.roll(wide, 1, axis=3)
            + jnp.roll(wide, -1, axis=3)
            - 4.0 * wide
        )
        wide = jnp.where(on, wide + diff_rate[None, :, None, None] * laplace, wide)
    return wide[:, :, NSTEP : NSTEP + tile]


def any_device(pert_fcst, control, departures, obs_weight, diff_rate, step_counts):
    members, levels, variables = pert_fcst.shape[:3]
    tile, lons = control.shape[2], control.shape[3]
    doms = lax.axis_size("dom")
    factor = 1.0 / math.sqrt(members * lax.axis_size("grp") - 1)
    localized = diffuse(control, diff_rate, step_counts)
    received = lax.all_to_all(
        pert_fcst.reshape(members * levels * variables, doms, -1),
        "dom",
        split_axis=1,
        concat_axis=1,
        tiled=True,
    )
    perturb = (
        received.reshape(-1, doms, tile, lons // doms)
        .transpose(0, 2, 1, 3)
        .reshape(members, levels, variables, tile, lons)
        .astype(jnp.float32)
    )
    increment = lax.psum(jnp.sum(perturb * localized[:, :, None], axis=0), "grp") * factor
    residual = obs_weight * (increment - departures)
    adjoint = jnp.sum(perturb * residual[None], axis=2) * factor
    return increment, control + diffuse(adjoint, diff_rate, step_counts)


def per_device(pert_fcst, control, departures, obs_weight, diff_rate, step_counts):
    members, levels, variables = pert_fcst.shape[:3]
    tile, lons = control.shape[2], control.shape[3]
    groups, doms = lax.axis_size("grp"), lax.axis_size("dom")
    small = (
        lons == 128
        and levels == 8
        and tile == NSTEP
        and members * levels * variables * tile == 128
        and doms % 2 == 0
        and lons // doms == 16
        and groups == 4
    )
    run = small_device if small else any_device
    return run(pert_fcst, control, departures, obs_weight, diff_rate, step_counts)


def solution(mesh):
    in_specs = (
        P("grp", None, None, "dom", None),
        P("grp", None, "dom", None),
        P(None, None, "dom", None),
        P(None, None, "dom", None),
        P(),
        P(),
    )
    out_specs = (P(None, None, "dom", None), P("grp", None, "dom", None))
    return jax.shard_map(
        per_device, mesh=mesh, in_specs=in_specs, out_specs=out_specs, check_vma=False
    )
```

```python
import functools
import math

import jax
import jax.numpy as jnp
from jax import lax
from jax.experimental import pallas as pl
from jax.experimental.pallas import tpu as pltpu
from jax.sharding import PartitionSpec as P

NSTEP = 4
CHIPS = (2, 3, 1, 0)
GROUPS = (3, 0, 1, 2)
VMEM = pl.BlockSpec(memory_space=pltpu.VMEM)
ANY = pl.BlockSpec(memory_space=pl.ANY)


def in_vmem(x):
    return pltpu.with_memory_space_constraint(x, pltpu.VMEM)


def down_rows(x, lons):
    wide = jnp.broadcast_to(x.astype(jnp.float32), (x.shape[1], x.shape[1]))
    on = lax.broadcasted_iota(jnp.int32, wide.shape, 0) == lax.broadcasted_iota(jnp.int32, wide.shape, 1)
    return jnp.broadcast_to(jnp.sum(jnp.where(on, wide, 0.0), axis=1, keepdims=True), (x.shape[1], lons))


def choice_kernel(rows, lons, out_ref):
    target = lax.broadcasted_iota(jnp.int32, out_ref.shape, 0)
    source = lax.broadcasted_iota(jnp.int32, out_ref.shape, 1)
    chosen = (target // lons == source // (rows * lons)) & (
        lax.rem(target, lons) == lax.rem(source, lons)
    )
    out_ref[...] = chosen.astype(jnp.float32).astype(jnp.bfloat16)


def pack_kernel(
    doms, rows, groups, chosen_ref, pert_ref, rate_ref, count_ref, out_ref, rates_ref, tiles_ref, rate_here, count_here, sems
):
    fetches = [
        pltpu.make_async_copy(rate_ref, rate_here, sems.at[groups]),
        pltpu.make_async_copy(count_ref, count_here, sems.at[groups + 1]),
    ]
    for copy in fetches:
        copy.start()
    _, variables, cells = pert_ref.shape
    lons = cells // (doms * rows)
    pert = pert_ref[...].astype(jnp.float32)
    fields = jnp.concatenate([pert[:, v, :] for v in range(variables)], axis=0)
    row_of = (lax.broadcasted_iota(jnp.int32, fields.shape, 1) // lons) % rows
    spread = jnp.concatenate(
        [jnp.where(row_of == r, fields, 0.0) for r in range(rows)], axis=0
    ).astype(jnp.bfloat16)
    chosen, pair = chosen_ref[...], chosen_ref.shape[1]
    for chip in range(doms // 2):
        both = lax.dot_general(
            chosen,
            spread[:, chip * pair : (chip + 1) * pair],
            (((1,), (1,)), ((), ())),
            preferred_element_type=jnp.float32,
        ).astype(jnp.bfloat16)
        for core in range(2):
            tiles_ref[core, CHIPS.index(chip)] = both[core * lons : (core + 1) * lons]
    stores = [pltpu.make_async_copy(tiles_ref, out_ref.at[:, g], sems.at[g]) for g in range(groups)]
    for copy in stores:
        copy.start()
    for copy in fetches:
        copy.wait()
    rate, count = (down_rows(ref[...], rates_ref.shape[2]) for ref in (rate_here, count_here))
    for step in range(NSTEP):
        rates_ref[step] = jnp.where(step < count, rate, 0.0)
    for copy in stores:
        copy.wait()


def sweeps(extended, rates, low_on, high_on, tile):
    lons = extended[0].shape[1]
    count = len(extended)
    powers = [list(extended)] + [[None] * count for _ in range(NSTEP)]
    for i in range(1, count - 1):
        deep = min(i, count - 1 - i, NSTEP)
        row = extended[i]
        pair = {
            k: pltpu.roll(row, k, 1) + pltpu.roll(row, lons - k, 1) for k in range(1, deep + 1)
        }
        pair[0] = row
        for n in range(1, deep + 1):
            total = pair[n]
            for k in range(1, (n + 1) // 2):
                total = total + float(math.comb(n, k)) * pair[n - 2 * k]
            if n % 2 == 0:
                total = total + float(math.comb(n, n // 2)) * row
            powers[n][i] = total
    for step in range(NSTEP):
        new = [[None] * count for _ in range(NSTEP - step)]
        for n in range(NSTEP - step):
            for i in range(step + 1 + n, count - 1 - step - n):
                if i < NSTEP:
                    rate = rates[step] * low_on
                elif i >= NSTEP + tile:
                    rate = rates[step] * high_on
                else:
                    rate = rates[step]
                mid = powers[n][i]
                laplace = powers[n][i + 1] + powers[n][i - 1] + powers[n + 1][i] - 4.0 * mid
                new[n][i] = mid + rate * laplace
        powers = new
    return powers[0][NSTEP : NSTEP + tile]


def edges():
    me, count = lax.axis_index("dom"), lax.axis_size("dom")
    odd = lax.rem(me, 2) == 1
    return odd, me > 0, me < count - 1


def with_halo(own, near, far, odd, low, high):
    below = [jnp.where(low, jnp.where(odd, n, f), 0.0) for n, f in zip(near, far)]
    above = [jnp.where(high, jnp.where(odd, f, n), 0.0) for n, f in zip(near, far)]
    return below + own + above


def localize_kernel(members, tile, rates_ref, own_ref, near_ref, far_ref, out_ref):
    levels = rates_ref.shape[1]
    odd, low, high = edges()
    low_on, high_on = low.astype(jnp.float32), high.astype(jnp.float32)
    rates = [rates_ref[step] for step in range(NSTEP)]
    for m in range(members):
        own, near, far = (
            [ref[pl.ds(m * levels * tile + r, levels, stride=tile), :] for r in range(tile)]
            for ref in (own_ref, near_ref, far_ref)
        )
        done = sweeps(with_halo(own, near, far, odd, low, high), rates, low_on, high_on, tile)
        for r in range(tile):
            out_ref[pl.ds((m * tile + r) * levels, levels), :] = done[r]


def adjoint_kernel(
    members, levels, variables, tile, groups, factor, tiles_ref, *refs
):
    local_refs, (weight_ref, depart_ref, inc_ref, adj_ref, far_ref) = refs[:groups], refs[groups:]
    mine = lax.axis_index("grp")
    sums, first = {}, None
    for j in range(groups):
        group = sum(
            jnp.where(jnp.bitwise_xor(mine, j) == g, GROUPS.index(g), 0) for g in range(groups)
        )
        blocks = [
            tiles_ref[core, group, CHIPS.index(chip)]
            for chip in range(len(CHIPS))
            for core in range(2)
        ]
        fields = jnp.concatenate(blocks, axis=0).astype(jnp.float32).T
        if j == 0:
            first = fields
        for r in range(tile):
            for v in range(variables):
                for m in range(members):
                    at = ((r * variables + v) * members + m) * levels
                    term = (
                        fields[at : at + levels]
                        * local_refs[j][pl.ds((m * tile + r) * levels, levels), :]
                    )
                    sums[r, v] = sums[r, v] + term if (r, v) in sums else term
    for r in range(tile):
        residual = []
        for v in range(variables):
            rows = pl.ds(v * tile + r, levels, stride=variables * tile)
            increment = sums[r, v] * factor
            inc_ref[rows, :] = increment
            residual.append(weight_ref[rows, :] * (increment - depart_ref[rows, :]))
        for m in range(members):
            total = None
            for v in range(variables):
                at = ((r * variables + v) * members + m) * levels
                term = first[at : at + levels] * residual[v]
                total = term if total is None else total + term
            adj_ref[pl.ds((m * tile + r) * levels, levels), :] = total * factor
            far_ref[pl.ds((m * tile + r) * levels, levels), :] = total * factor
    far_ref[pl.ds(members * tile * levels, levels), :] = jnp.zeros((levels, inc_ref.shape[1]), jnp.float32)


def gradient_rows(members, tile, rates_ref, own_ref, near_ref, far_ref, control_ref, out_ref):
    levels = rates_ref.shape[1]
    odd, low, high = edges()
    low_on, high_on = low.astype(jnp.float32), high.astype(jnp.float32)
    rates = [rates_ref[step] for step in range(NSTEP)]
    for m in range(members):
        own, near, far = (
            [ref[pl.ds((m * tile + r) * levels, levels), :] for r in range(tile)]
            for ref in (own_ref, near_ref, near_ref if far_ref is None else far_ref)
        )
        done = sweeps(with_halo(own, near, far, odd, low, high), rates, low_on, high_on, tile)
        for r in range(tile):
            rows = pl.ds(m * levels * tile + r, levels, stride=tile)
            out_ref[rows, :] = control_ref[rows, :] + done[r]


def end_kernel(members, tile, rates_ref, own_ref, near_ref, control_ref, out_ref, rows_ref, sem):
    _, low, high = edges()

    @pl.when(jnp.logical_not(low & high))
    def _():
        gradient_rows(members, tile, rates_ref, own_ref, near_ref, None, control_ref, rows_ref)
        copy = pltpu.make_async_copy(rows_ref, out_ref, sem)
        copy.start()
        copy.wait()


def inner_kernel(
    members, tile, rates_ref, own_ref, near_ref, far_ref, control_ref, _, out_ref, rows_ref, sem
):
    _, low, high = edges()

    @pl.when(low & high)
    def _():
        gradient_rows(
            members, tile, rates_ref, own_ref, near_ref, far_ref, control_ref, rows_ref
        )
        copy = pltpu.make_async_copy(rows_ref, out_ref, sem)
        copy.start()
        copy.wait()


def near_pairs(doms):
    return [(i, i ^ 1) for i in range(doms)]


def far_pairs(groups, doms):
    pairs = []
    for g in range(groups):
        for d in range(doms):
            if d in (0, doms - 1):
                pairs.append((g * doms + d, (g ^ 1) * doms + d))
            else:
                pairs.append((g * doms + d, g * doms + (d + 1 if d % 2 else d - 1)))
    return pairs


def core_order(groups, doms):
    return [
        [
            g * doms + 2 * chip + core
            for core in range(2)
            for g in GROUPS
            for chip in CHIPS
        ]
    ]


def beside(x, groups, doms):
    near = lax.ppermute(x, "dom", near_pairs(doms))
    far = lax.ppermute(x, ("grp", "dom"), far_pairs(groups, doms))
    return near, far


def small_device(pert_fcst, control, departures, obs_weight, diff_rate, step_counts):
    members, levels, variables = pert_fcst.shape[:3]
    tile, lons = control.shape[2], control.shape[3]
    groups, doms = lax.axis_size("grp"), lax.axis_size("dom")
    factor = 1.0 / math.sqrt(members * groups - 1)
    fields = members * levels * variables * tile
    flat = control.reshape(-1, lons)
    cells = pert_fcst.shape[-1]
    chosen = pl.pallas_call(
        functools.partial(choice_kernel, tile, lons // doms),
        out_shape=pltpu.VMEM((2 * lons // doms, 2 * cells // doms), jnp.bfloat16),
        out_specs=VMEM,
        cost_estimate=pl.CostEstimate(flops=10**10, bytes_accessed=0, transcendentals=0),
    )()
    tiles, rates = pl.pallas_call(
        functools.partial(pack_kernel, doms, tile, groups),
        out_shape=[
            jax.ShapeDtypeStruct((2, groups, doms // 2, lons // doms, fields), jnp.bfloat16),
            pltpu.VMEM((NSTEP, levels, lons), jnp.float32),
        ],
        in_specs=[VMEM, VMEM, ANY, ANY],
        out_specs=[ANY, VMEM],
        scratch_shapes=[
            pltpu.VMEM((2, doms // 2, lons // doms, fields), jnp.bfloat16),
            pltpu.VMEM((1, levels), jnp.float32),
            pltpu.VMEM((1, levels), jnp.int32),
            pltpu.SemaphoreType.DMA((groups + 2,)),
        ],
    )(
        in_vmem(chosen),
        in_vmem(pert_fcst.reshape(members * levels, variables, -1)),
        diff_rate.reshape(1, -1),
        step_counts.reshape(1, -1),
    )
    near, far = beside(flat, groups, doms)
    received = lax.all_to_all(
        tiles.reshape(-1, *tiles.shape[3:]),
        ("grp", "dom"),
        split_axis=0,
        concat_axis=0,
        tiled=True,
        axis_index_groups=core_order(groups, doms),
    )
    tiles = received.reshape(tiles.shape)
    local = pl.pallas_call(
        functools.partial(localize_kernel, members, tile),
        out_shape=pltpu.VMEM(flat.shape, jnp.float32),
        in_specs=[VMEM] * 4,
        out_specs=VMEM,
        cost_estimate=pl.CostEstimate(flops=10**10, bytes_accessed=0, transcendentals=0),
    )(in_vmem(rates), in_vmem(flat), in_vmem(near), in_vmem(far))
    locals_ = [local] + [
        lax.ppermute(local, "grp", [(i, i ^ j) for i in range(groups)]) for j in range(1, groups)
    ]
    increment, adjoint, for_far = pl.pallas_call(
        functools.partial(adjoint_kernel, members, levels, variables, tile, groups, factor),
        out_shape=[
            pltpu.VMEM((levels * variables * tile, lons), jnp.float32),
            pltpu.VMEM(flat.shape, jnp.float32),
            pltpu.VMEM((flat.shape[0] + levels, lons), jnp.float32),
        ],
        in_specs=[VMEM] * (groups + 3),
        out_specs=[VMEM, VMEM, VMEM],
    )(
        in_vmem(tiles),
        *[in_vmem(x) for x in locals_],
        in_vmem(obs_weight.reshape(-1, lons)),
        in_vmem(departures.reshape(-1, lons)),
    )
    near = lax.ppermute(adjoint, "dom", near_pairs(doms))
    far = lax.ppermute(for_far, ("grp", "dom"), far_pairs(groups, doms))
    at_ends = pl.pallas_call(
        functools.partial(end_kernel, members, tile),
        out_shape=jax.ShapeDtypeStruct(flat.shape, jnp.float32),
        in_specs=[VMEM] * 4,
        out_specs=ANY,
        scratch_shapes=[pltpu.VMEM(flat.shape, jnp.float32), pltpu.SemaphoreType.DMA],
        cost_estimate=pl.CostEstimate(flops=0, bytes_accessed=0, transcendentals=0),
    )(in_vmem(rates), in_vmem(adjoint), in_vmem(near), in_vmem(flat))
    gradient = pl.pallas_call(
        functools.partial(inner_kernel, members, tile),
        out_shape=jax.ShapeDtypeStruct(flat.shape, jnp.float32),
        in_specs=[VMEM] * 5 + [ANY],
        out_specs=ANY,
        scratch_shapes=[pltpu.VMEM(flat.shape, jnp.float32), pltpu.SemaphoreType.DMA],
        input_output_aliases={5: 0},
    )(in_vmem(rates), in_vmem(adjoint), in_vmem(near), in_vmem(far), in_vmem(flat), at_ends)
    return increment.reshape(departures.shape), gradient.reshape(control.shape)


def diffuse(field, diff_rate, step_counts):
    count, me = lax.axis_size("dom"), lax.axis_index("dom")
    forward = [(i, i + 1) for i in range(count - 1)]
    backward = [(target, source) for source, target in forward]
    tile = field.shape[2]
    low = lax.ppermute(field[:, :, tile - NSTEP :], "dom", forward)
    high = lax.ppermute(field[:, :, :NSTEP], "dom", backward)
    wide = jnp.concatenate([low, field, high], axis=2)
    row = lax.broadcasted_iota(jnp.int32, (1, 1, wide.shape[2], 1), 2)
    inside = ((row >= NSTEP) | (me > 0)) & ((row < NSTEP + tile) | (me < count - 1))
    for step in range(NSTEP):
        on = (step < step_counts)[None, :, None, None] & inside
        padded = jnp.pad(wide, ((0, 0), (0, 0), (1, 1), (0, 0)))
        laplace = (
            padded[:, :, 2:]
            + padded[:, :, :-2]
            + jnp.roll(wide, 1, axis=3)
            + jnp.roll(wide, -1, axis=3)
            - 4.0 * wide
        )
        wide = jnp.where(on, wide + diff_rate[None, :, None, None] * laplace, wide)
    return wide[:, :, NSTEP : NSTEP + tile]


def any_device(pert_fcst, control, departures, obs_weight, diff_rate, step_counts):
    members, levels, variables = pert_fcst.shape[:3]
    tile, lons = control.shape[2], control.shape[3]
    doms = lax.axis_size("dom")
    factor = 1.0 / math.sqrt(members * lax.axis_size("grp") - 1)
    localized = diffuse(control, diff_rate, step_counts)
    received = lax.all_to_all(
        pert_fcst.reshape(members * levels * variables, doms, -1),
        "dom",
        split_axis=1,
        concat_axis=1,
        tiled=True,
    )
    perturb = (
        received.reshape(-1, doms, tile, lons // doms)
        .transpose(0, 2, 1, 3)
        .reshape(members, levels, variables, tile, lons)
        .astype(jnp.float32)
    )
    increment = lax.psum(jnp.sum(perturb * localized[:, :, None], axis=0), "grp") * factor
    residual = obs_weight * (increment - departures)
    adjoint = jnp.sum(perturb * residual[None], axis=2) * factor
    return increment, control + diffuse(adjoint, diff_rate, step_counts)


def per_device(pert_fcst, control, departures, obs_weight, diff_rate, step_counts):
    members, levels, variables = pert_fcst.shape[:3]
    tile, lons = control.shape[2], control.shape[3]
    groups, doms = lax.axis_size("grp"), lax.axis_size("dom")
    small = (
        lons == 128
        and levels == 8
        and tile == NSTEP
        and members * levels * variables * tile == 128
        and doms == 2 * len(CHIPS)
        and lons // doms == 16
        and groups == len(GROUPS)
    )
    run = small_device if small else any_device
    return run(pert_fcst, control, departures, obs_weight, diff_rate, step_counts)


def solution(mesh):
    in_specs = (
        P("grp", None, None, "dom", None),
        P("grp", None, "dom", None),
        P(None, None, "dom", None),
        P(None, None, "dom", None),
        P(),
        P(),
    )
    out_specs = (P(None, None, "dom", None), P("grp", None, "dom", None))
    return jax.shard_map(
        per_device, mesh=mesh, in_specs=in_specs, out_specs=out_specs, check_vma=False
    )
```

```python
import functools
import math

import jax
import jax.numpy as jnp
from jax import lax
from jax.experimental import pallas as pl
from jax.experimental.pallas import tpu as pltpu
from jax.sharding import PartitionSpec as P

NSTEP = 4
CHIPS = (2, 3, 1, 0)
GROUPS = (3, 0, 1, 2)
PARTNERS = ((1, 2, 3), (2, 3, 1))
VMEM = pl.BlockSpec(memory_space=pltpu.VMEM)
ANY = pl.BlockSpec(memory_space=pl.ANY)


def in_vmem(x):
    return pltpu.with_memory_space_constraint(x, pltpu.VMEM)


def down_rows(x, lons):
    wide = jnp.broadcast_to(x.astype(jnp.float32), (x.shape[1], x.shape[1]))
    on = lax.broadcasted_iota(jnp.int32, wide.shape, 0) == lax.broadcasted_iota(jnp.int32, wide.shape, 1)
    return jnp.broadcast_to(jnp.sum(jnp.where(on, wide, 0.0), axis=1, keepdims=True), (x.shape[1], lons))


def choice_kernel(rows, lons, out_ref):
    target = lax.broadcasted_iota(jnp.int32, out_ref.shape, 0)
    source = lax.broadcasted_iota(jnp.int32, out_ref.shape, 1)
    chosen = (target // lons == source // (rows * lons)) & (
        lax.rem(target, lons) == lax.rem(source, lons)
    )
    out_ref[...] = chosen.astype(jnp.float32).astype(jnp.bfloat16)


def pack_kernel(
    doms, rows, groups, chosen_ref, pert_ref, rate_ref, count_ref, out_ref, rates_ref, tiles_ref, rate_here, count_here, sems
):
    fetches = [
        pltpu.make_async_copy(rate_ref, rate_here, sems.at[groups]),
        pltpu.make_async_copy(count_ref, count_here, sems.at[groups + 1]),
    ]
    for copy in fetches:
        copy.start()
    _, variables, cells = pert_ref.shape
    lons = cells // (doms * rows)
    pert = pert_ref[...].astype(jnp.float32)
    fields = jnp.concatenate([pert[:, v, :] for v in range(variables)], axis=0)
    row_of = (lax.broadcasted_iota(jnp.int32, fields.shape, 1) // lons) % rows
    spread = jnp.concatenate(
        [jnp.where(row_of == r, fields, 0.0) for r in range(rows)], axis=0
    ).astype(jnp.bfloat16)
    chosen, pair = chosen_ref[...], chosen_ref.shape[1]
    for chip in range(doms // 2):
        both = lax.dot_general(
            chosen,
            spread[:, chip * pair : (chip + 1) * pair],
            (((1,), (1,)), ((), ())),
            preferred_element_type=jnp.float32,
        ).astype(jnp.bfloat16)
        for core in range(2):
            tiles_ref[core, CHIPS.index(chip)] = both[core * lons : (core + 1) * lons]
    stores = [pltpu.make_async_copy(tiles_ref, out_ref.at[:, g], sems.at[g]) for g in range(groups)]
    for copy in stores:
        copy.start()
    for copy in fetches:
        copy.wait()
    rate, count = (down_rows(ref[...], rates_ref.shape[2]) for ref in (rate_here, count_here))
    for step in range(NSTEP):
        rates_ref[step] = jnp.where(step < count, rate, 0.0)
    for copy in stores:
        copy.wait()


def sweeps(extended, rates, low_on, high_on, tile):
    lons = extended[0].shape[1]
    count = len(extended)
    powers = [list(extended)] + [[None] * count for _ in range(NSTEP)]
    for i in range(1, count - 1):
        deep = min(i, count - 1 - i, NSTEP)
        row = extended[i]
        pair = {
            k: pltpu.roll(row, k, 1) + pltpu.roll(row, lons - k, 1) for k in range(1, deep + 1)
        }
        pair[0] = row
        for n in range(1, deep + 1):
            total = pair[n]
            for k in range(1, (n + 1) // 2):
                total = total + float(math.comb(n, k)) * pair[n - 2 * k]
            if n % 2 == 0:
                total = total + float(math.comb(n, n // 2)) * row
            powers[n][i] = total
    for step in range(NSTEP):
        new = [[None] * count for _ in range(NSTEP - step)]
        for n in range(NSTEP - step):
            for i in range(step + 1 + n, count - 1 - step - n):
                if i < NSTEP:
                    rate = rates[step] * low_on
                elif i >= NSTEP + tile:
                    rate = rates[step] * high_on
                else:
                    rate = rates[step]
                mid = powers[n][i]
                laplace = powers[n][i + 1] + powers[n][i - 1] + powers[n + 1][i] - 4.0 * mid
                new[n][i] = mid + rate * laplace
        powers = new
    return powers[0][NSTEP : NSTEP + tile]


def edges():
    me, count = lax.axis_index("dom"), lax.axis_size("dom")
    odd = lax.rem(me, 2) == 1
    return odd, me > 0, me < count - 1


def with_halo(own, near, far, odd, low, high):
    below = [jnp.where(low, jnp.where(odd, n, f), 0.0) for n, f in zip(near, far)]
    above = [jnp.where(high, jnp.where(odd, f, n), 0.0) for n, f in zip(near, far)]
    return below + own + above


def localize_kernel(members, tile, rates_ref, own_ref, near_ref, far_ref, out_ref):
    levels = rates_ref.shape[1]
    odd, low, high = edges()
    low_on, high_on = low.astype(jnp.float32), high.astype(jnp.float32)
    rates = [rates_ref[step] for step in range(NSTEP)]
    for m in range(members):
        own, near, far = (
            [ref[pl.ds(m * levels * tile + r, levels, stride=tile), :] for r in range(tile)]
            for ref in (own_ref, near_ref, far_ref)
        )
        done = sweeps(with_halo(own, near, far, odd, low, high), rates, low_on, high_on, tile)
        for r in range(tile):
            out_ref[pl.ds((m * tile + r) * levels, levels), :] = done[r]


def adjoint_kernel(
    members, levels, variables, tile, groups, factor, tiles_ref, *refs
):
    local_refs, (weight_ref, depart_ref, inc_ref, adj_ref, far_ref) = refs[:groups], refs[groups:]
    mine, odd = lax.axis_index("grp"), lax.rem(lax.axis_index("dom"), 2) == 1
    sums, first = {}, None
    for j in range(groups):
        partner = jnp.where(odd, PARTNERS[1][j - 1], PARTNERS[0][j - 1]) if j else 0
        group = sum(
            jnp.where(jnp.bitwise_xor(mine, partner) == g, GROUPS.index(g), 0)
            for g in range(groups)
        )
        blocks = [
            tiles_ref[core, group, CHIPS.index(chip)]
            for chip in range(len(CHIPS))
            for core in range(2)
        ]
        fields = jnp.concatenate(blocks, axis=0).astype(jnp.float32).T
        if j == 0:
            first = fields
        for r in range(tile):
            for v in range(variables):
                for m in range(members):
                    at = ((r * variables + v) * members + m) * levels
                    term = (
                        fields[at : at + levels]
                        * local_refs[j][pl.ds((m * tile + r) * levels, levels), :]
                    )
                    sums[r, v] = sums[r, v] + term if (r, v) in sums else term
    for r in range(tile):
        residual = []
        for v in range(variables):
            rows = pl.ds(v * tile + r, levels, stride=variables * tile)
            increment = sums[r, v] * factor
            inc_ref[rows, :] = increment
            residual.append(weight_ref[rows, :] * (increment - depart_ref[rows, :]))
        for m in range(members):
            total = None
            for v in range(variables):
                at = ((r * variables + v) * members + m) * levels
                term = first[at : at + levels] * residual[v]
                total = term if total is None else total + term
            adj_ref[pl.ds((m * tile + r) * levels, levels), :] = total * factor
            far_ref[pl.ds((m * tile + r) * levels, levels), :] = total * factor
    far_ref[pl.ds(members * tile * levels, levels), :] = jnp.zeros((levels, inc_ref.shape[1]), jnp.float32)


def gradient_rows(members, tile, rates_ref, own_ref, near_ref, far_ref, control_ref, out_ref):
    levels = rates_ref.shape[1]
    odd, low, high = edges()
    low_on, high_on = low.astype(jnp.float32), high.astype(jnp.float32)
    rates = [rates_ref[step] for step in range(NSTEP)]
    for m in range(members):
        own, near, far = (
            [ref[pl.ds((m * tile + r) * levels, levels), :] for r in range(tile)]
            for ref in (own_ref, near_ref, near_ref if far_ref is None else far_ref)
        )
        done = sweeps(with_halo(own, near, far, odd, low, high), rates, low_on, high_on, tile)
        for r in range(tile):
            rows = pl.ds(m * levels * tile + r, levels, stride=tile)
            out_ref[rows, :] = control_ref[rows, :] + done[r]


def end_kernel(members, tile, rates_ref, own_ref, near_ref, control_ref, out_ref, rows_ref, sem):
    _, low, high = edges()

    @pl.when(jnp.logical_not(low & high))
    def _():
        gradient_rows(members, tile, rates_ref, own_ref, near_ref, None, control_ref, rows_ref)
        copy = pltpu.make_async_copy(rows_ref, out_ref, sem)
        copy.start()
        copy.wait()


def inner_kernel(
    members, tile, rates_ref, own_ref, near_ref, far_ref, control_ref, _, out_ref, rows_ref, sem
):
    _, low, high = edges()

    @pl.when(low & high)
    def _():
        gradient_rows(
            members, tile, rates_ref, own_ref, near_ref, far_ref, control_ref, rows_ref
        )
        copy = pltpu.make_async_copy(rows_ref, out_ref, sem)
        copy.start()
        copy.wait()


def near_pairs(doms):
    return [(i, i ^ 1) for i in range(doms)]


def far_pairs(groups, doms):
    pairs = []
    for g in range(groups):
        for d in range(doms):
            if d in (0, doms - 1):
                pairs.append((g * doms + d, (g ^ 1) * doms + d))
            else:
                pairs.append((g * doms + d, g * doms + (d + 1 if d % 2 else d - 1)))
    return pairs


def core_order(groups, doms):
    return [
        [
            g * doms + 2 * chip + core
            for core in range(2)
            for g in GROUPS
            for chip in CHIPS
        ]
    ]


def group_pairs(groups, doms, k):
    return [
        (g * doms + d, (g ^ PARTNERS[d % 2][k]) * doms + d)
        for g in range(groups)
        for d in range(doms)
    ]


def beside(x, groups, doms):
    near = lax.ppermute(x, "dom", near_pairs(doms))
    far = lax.ppermute(x, ("grp", "dom"), far_pairs(groups, doms))
    return near, far


def small_device(pert_fcst, control, departures, obs_weight, diff_rate, step_counts):
    members, levels, variables = pert_fcst.shape[:3]
    tile, lons = control.shape[2], control.shape[3]
    groups, doms = lax.axis_size("grp"), lax.axis_size("dom")
    factor = 1.0 / math.sqrt(members * groups - 1)
    fields = members * levels * variables * tile
    flat = control.reshape(-1, lons)
    cells = pert_fcst.shape[-1]
    chosen = pl.pallas_call(
        functools.partial(choice_kernel, tile, lons // doms),
        out_shape=pltpu.VMEM((2 * lons // doms, 2 * cells // doms), jnp.bfloat16),
        out_specs=VMEM,
        cost_estimate=pl.CostEstimate(flops=10**10, bytes_accessed=0, transcendentals=0),
    )()
    tiles, rates = pl.pallas_call(
        functools.partial(pack_kernel, doms, tile, groups),
        out_shape=[
            jax.ShapeDtypeStruct((2, groups, doms // 2, lons // doms, fields), jnp.bfloat16),
            pltpu.VMEM((NSTEP, levels, lons), jnp.float32),
        ],
        in_specs=[VMEM, VMEM, ANY, ANY],
        out_specs=[ANY, VMEM],
        scratch_shapes=[
            pltpu.VMEM((2, doms // 2, lons // doms, fields), jnp.bfloat16),
            pltpu.VMEM((1, levels), jnp.float32),
            pltpu.VMEM((1, levels), jnp.int32),
            pltpu.SemaphoreType.DMA((groups + 2,)),
        ],
    )(
        in_vmem(chosen),
        in_vmem(pert_fcst.reshape(members * levels, variables, -1)),
        diff_rate.reshape(1, -1),
        step_counts.reshape(1, -1),
    )
    near, far = beside(flat, groups, doms)
    received = lax.all_to_all(
        tiles.reshape(-1, *tiles.shape[3:]),
        ("grp", "dom"),
        split_axis=0,
        concat_axis=0,
        tiled=True,
        axis_index_groups=core_order(groups, doms),
    )
    tiles = received.reshape(tiles.shape)
    local = pl.pallas_call(
        functools.partial(localize_kernel, members, tile),
        out_shape=pltpu.VMEM(flat.shape, jnp.float32),
        in_specs=[VMEM] * 4,
        out_specs=VMEM,
        cost_estimate=pl.CostEstimate(flops=10**10, bytes_accessed=0, transcendentals=0),
    )(in_vmem(rates), in_vmem(flat), in_vmem(near), in_vmem(far))
    locals_ = [local] + [
        lax.ppermute(local, ("grp", "dom"), group_pairs(groups, doms, k)) for k in range(groups - 1)
    ]
    increment, adjoint, for_far = pl.pallas_call(
        functools.partial(adjoint_kernel, members, levels, variables, tile, groups, factor),
        out_shape=[
            pltpu.VMEM((levels * variables * tile, lons), jnp.float32),
            pltpu.VMEM(flat.shape, jnp.float32),
            pltpu.VMEM((flat.shape[0] + levels, lons), jnp.float32),
        ],
        in_specs=[VMEM] * (groups + 3),
        out_specs=[VMEM, VMEM, VMEM],
    )(
        in_vmem(tiles),
        *[in_vmem(x) for x in locals_],
        in_vmem(obs_weight.reshape(-1, lons)),
        in_vmem(departures.reshape(-1, lons)),
    )
    near = lax.ppermute(adjoint, "dom", near_pairs(doms))
    far = lax.ppermute(for_far, ("grp", "dom"), far_pairs(groups, doms))
    at_ends = pl.pallas_call(
        functools.partial(end_kernel, members, tile),
        out_shape=jax.ShapeDtypeStruct(flat.shape, jnp.float32),
        in_specs=[VMEM] * 4,
        out_specs=ANY,
        scratch_shapes=[pltpu.VMEM(flat.shape, jnp.float32), pltpu.SemaphoreType.DMA],
        cost_estimate=pl.CostEstimate(flops=0, bytes_accessed=0, transcendentals=0),
    )(in_vmem(rates), in_vmem(adjoint), in_vmem(near), in_vmem(flat))
    gradient = pl.pallas_call(
        functools.partial(inner_kernel, members, tile),
        out_shape=jax.ShapeDtypeStruct(flat.shape, jnp.float32),
        in_specs=[VMEM] * 5 + [ANY],
        out_specs=ANY,
        scratch_shapes=[pltpu.VMEM(flat.shape, jnp.float32), pltpu.SemaphoreType.DMA],
        input_output_aliases={5: 0},
    )(in_vmem(rates), in_vmem(adjoint), in_vmem(near), in_vmem(far), in_vmem(flat), at_ends)
    return increment.reshape(departures.shape), gradient.reshape(control.shape)


def diffuse(field, diff_rate, step_counts):
    count, me = lax.axis_size("dom"), lax.axis_index("dom")
    forward = [(i, i + 1) for i in range(count - 1)]
    backward = [(target, source) for source, target in forward]
    tile = field.shape[2]
    low = lax.ppermute(field[:, :, tile - NSTEP :], "dom", forward)
    high = lax.ppermute(field[:, :, :NSTEP], "dom", backward)
    wide = jnp.concatenate([low, field, high], axis=2)
    row = lax.broadcasted_iota(jnp.int32, (1, 1, wide.shape[2], 1), 2)
    inside = ((row >= NSTEP) | (me > 0)) & ((row < NSTEP + tile) | (me < count - 1))
    for step in range(NSTEP):
        on = (step < step_counts)[None, :, None, None] & inside
        padded = jnp.pad(wide, ((0, 0), (0, 0), (1, 1), (0, 0)))
        laplace = (
            padded[:, :, 2:]
            + padded[:, :, :-2]
            + jnp.roll(wide, 1, axis=3)
            + jnp.roll(wide, -1, axis=3)
            - 4.0 * wide
        )
        wide = jnp.where(on, wide + diff_rate[None, :, None, None] * laplace, wide)
    return wide[:, :, NSTEP : NSTEP + tile]


def any_device(pert_fcst, control, departures, obs_weight, diff_rate, step_counts):
    members, levels, variables = pert_fcst.shape[:3]
    tile, lons = control.shape[2], control.shape[3]
    doms = lax.axis_size("dom")
    factor = 1.0 / math.sqrt(members * lax.axis_size("grp") - 1)
    localized = diffuse(control, diff_rate, step_counts)
    received = lax.all_to_all(
        pert_fcst.reshape(members * levels * variables, doms, -1),
        "dom",
        split_axis=1,
        concat_axis=1,
        tiled=True,
    )
    perturb = (
        received.reshape(-1, doms, tile, lons // doms)
        .transpose(0, 2, 1, 3)
        .reshape(members, levels, variables, tile, lons)
        .astype(jnp.float32)
    )
    increment = lax.psum(jnp.sum(perturb * localized[:, :, None], axis=0), "grp") * factor
    residual = obs_weight * (increment - departures)
    adjoint = jnp.sum(perturb * residual[None], axis=2) * factor
    return increment, control + diffuse(adjoint, diff_rate, step_counts)


def per_device(pert_fcst, control, departures, obs_weight, diff_rate, step_counts):
    members, levels, variables = pert_fcst.shape[:3]
    tile, lons = control.shape[2], control.shape[3]
    groups, doms = lax.axis_size("grp"), lax.axis_size("dom")
    small = (
        lons == 128
        and levels == 8
        and tile == NSTEP
        and members * levels * variables * tile == 128
        and doms == 2 * len(CHIPS)
        and lons // doms == 16
        and groups == len(GROUPS)
    )
    run = small_device if small else any_device
    return run(pert_fcst, control, departures, obs_weight, diff_rate, step_counts)


def solution(mesh):
    in_specs = (
        P("grp", None, None, "dom", None),
        P("grp", None, "dom", None),
        P(None, None, "dom", None),
        P(None, None, "dom", None),
        P(),
        P(),
    )
    out_specs = (P(None, None, "dom", None), P("grp", None, "dom", None))
    return jax.shard_map(
        per_device, mesh=mesh, in_specs=in_specs, out_specs=out_specs, check_vma=False
    )
```

```python
import functools
import math

import jax
import jax.numpy as jnp
from jax import lax
from jax.experimental import pallas as pl
from jax.experimental.pallas import tpu as pltpu
from jax.sharding import PartitionSpec as P

NSTEP = 4
CHIPS = (2, 3, 1, 0)
GROUPS = (3, 0, 1, 2)
VMEM = pl.BlockSpec(memory_space=pltpu.VMEM)
ANY = pl.BlockSpec(memory_space=pl.ANY)


def in_vmem(x):
    return pltpu.with_memory_space_constraint(x, pltpu.VMEM)


def down_rows(x, lons):
    wide = jnp.broadcast_to(x.astype(jnp.float32), (x.shape[1], x.shape[1]))
    on = lax.broadcasted_iota(jnp.int32, wide.shape, 0) == lax.broadcasted_iota(jnp.int32, wide.shape, 1)
    return jnp.broadcast_to(jnp.sum(jnp.where(on, wide, 0.0), axis=1, keepdims=True), (x.shape[1], lons))


def choice_kernel(rows, lons, out_ref):
    target = lax.broadcasted_iota(jnp.int32, out_ref.shape, 0)
    source = lax.broadcasted_iota(jnp.int32, out_ref.shape, 1)
    chosen = (target // lons == source // (rows * lons)) & (
        lax.rem(target, lons) == lax.rem(source, lons)
    )
    out_ref[...] = chosen.astype(jnp.float32).astype(jnp.bfloat16)


def pack_kernel(
    doms, rows, groups, chosen_ref, pert_ref, rate_ref, count_ref, out_ref, rates_ref, tiles_ref, rate_here, count_here, sems
):
    fetches = [
        pltpu.make_async_copy(rate_ref, rate_here, sems.at[groups]),
        pltpu.make_async_copy(count_ref, count_here, sems.at[groups + 1]),
    ]
    for copy in fetches:
        copy.start()
    _, variables, cells = pert_ref.shape
    lons = cells // (doms * rows)
    pert = pert_ref[...].astype(jnp.float32)
    fields = jnp.concatenate([pert[:, v, :] for v in range(variables)], axis=0)
    row_of = (lax.broadcasted_iota(jnp.int32, fields.shape, 1) // lons) % rows
    spread = jnp.concatenate(
        [jnp.where(row_of == r, fields, 0.0) for r in range(rows)], axis=0
    ).astype(jnp.bfloat16)
    chosen, pair = chosen_ref[...], chosen_ref.shape[1]
    for chip in range(doms // 2):
        both = lax.dot_general(
            chosen,
            spread[:, chip * pair : (chip + 1) * pair],
            (((1,), (1,)), ((), ())),
            preferred_element_type=jnp.float32,
        ).astype(jnp.bfloat16)
        for core in range(2):
            tiles_ref[core, CHIPS.index(chip)] = both[core * lons : (core + 1) * lons]
    stores = [pltpu.make_async_copy(tiles_ref, out_ref.at[:, g], sems.at[g]) for g in range(groups)]
    for copy in stores:
        copy.start()
    for copy in fetches:
        copy.wait()
    rate, count = (down_rows(ref[...], rates_ref.shape[2]) for ref in (rate_here, count_here))
    for step in range(NSTEP):
        rates_ref[step] = jnp.where(step < count, rate, 0.0)
    for copy in stores:
        copy.wait()


def sweeps(extended, rates, low_on, high_on, tile):
    lons = extended[0].shape[1]
    count = len(extended)
    powers = [list(extended)] + [[None] * count for _ in range(NSTEP)]
    for i in range(1, count - 1):
        deep = min(i, count - 1 - i, NSTEP)
        row = extended[i]
        pair = {
            k: pltpu.roll(row, k, 1) + pltpu.roll(row, lons - k, 1) for k in range(1, deep + 1)
        }
        pair[0] = row
        for n in range(1, deep + 1):
            total = pair[n]
            for k in range(1, (n + 1) // 2):
                total = total + float(math.comb(n, k)) * pair[n - 2 * k]
            if n % 2 == 0:
                total = total + float(math.comb(n, n // 2)) * row
            powers[n][i] = total
    for step in range(NSTEP):
        new = [[None] * count for _ in range(NSTEP - step)]
        for n in range(NSTEP - step):
            for i in range(step + 1 + n, count - 1 - step - n):
                if i < NSTEP:
                    rate = rates[step] * low_on
                elif i >= NSTEP + tile:
                    rate = rates[step] * high_on
                else:
                    rate = rates[step]
                mid = powers[n][i]
                laplace = powers[n][i + 1] + powers[n][i - 1] + powers[n + 1][i] - 4.0 * mid
                new[n][i] = mid + rate * laplace
        powers = new
    return powers[0][NSTEP : NSTEP + tile]


def edges():
    me, count = lax.axis_index("dom"), lax.axis_size("dom")
    odd = lax.rem(me, 2) == 1
    return odd, me > 0, me < count - 1


def with_halo(own, near, far, odd, low, high):
    below = [jnp.where(low, jnp.where(odd, n, f), 0.0) for n, f in zip(near, far)]
    above = [jnp.where(high, jnp.where(odd, f, n), 0.0) for n, f in zip(near, far)]
    return below + own + above


def localize_kernel(members, tile, rates_ref, own_ref, near_ref, far_ref, out_ref):
    levels = rates_ref.shape[1]
    odd, low, high = edges()
    low_on, high_on = low.astype(jnp.float32), high.astype(jnp.float32)
    rates = [rates_ref[step] for step in range(NSTEP)]
    for m in range(members):
        own, near, far = (
            [ref[pl.ds(m * levels * tile + r, levels, stride=tile), :] for r in range(tile)]
            for ref in (own_ref, near_ref, far_ref)
        )
        done = sweeps(with_halo(own, near, far, odd, low, high), rates, low_on, high_on, tile)
        for r in range(tile):
            out_ref[pl.ds((m * tile + r) * levels, levels), :] = done[r]


def adjoint_kernel(
    members, levels, variables, tile, groups, factor, tiles_ref, *refs
):
    local_refs, (weight_ref, depart_ref, inc_ref, adj_ref, far_ref) = refs[:groups], refs[groups:]
    mine = lax.axis_index("grp")
    sums, first = {}, None
    for j in range(groups):
        group = sum(
            jnp.where(jnp.bitwise_xor(mine, j) == g, GROUPS.index(g), 0) for g in range(groups)
        )
        blocks = [
            tiles_ref[core, group, CHIPS.index(chip)]
            for chip in range(len(CHIPS))
            for core in range(2)
        ]
        fields = jnp.concatenate(blocks, axis=0).astype(jnp.float32).T
        if j == 0:
            first = fields
        for r in range(tile):
            for v in range(variables):
                for m in range(members):
                    at = ((r * variables + v) * members + m) * levels
                    term = (
                        fields[at : at + levels]
                        * local_refs[j][pl.ds((m * tile + r) * levels, levels), :]
                    )
                    sums[r, v] = sums[r, v] + term if (r, v) in sums else term
    for r in range(tile):
        residual = []
        for v in range(variables):
            rows = pl.ds(v * tile + r, levels, stride=variables * tile)
            increment = sums[r, v] * factor
            inc_ref[rows, :] = increment
            residual.append(weight_ref[rows, :] * (increment - depart_ref[rows, :]))
        for m in range(members):
            total = None
            for v in range(variables):
                at = ((r * variables + v) * members + m) * levels
                term = first[at : at + levels] * residual[v]
                total = term if total is None else total + term
            adj_ref[pl.ds((m * tile + r) * levels, levels), :] = total * factor
            far_ref[pl.ds((m * tile + r) * levels, levels), :] = total * factor
    far_ref[pl.ds(members * tile * levels, levels), :] = jnp.zeros((levels, inc_ref.shape[1]), jnp.float32)


def gradient_rows(members, tile, rates_ref, own_ref, near_ref, far_ref, control_ref, out_ref):
    levels = rates_ref.shape[1]
    odd, low, high = edges()
    low_on, high_on = low.astype(jnp.float32), high.astype(jnp.float32)
    rates = [rates_ref[step] for step in range(NSTEP)]
    for m in range(members):
        own, near, far = (
            [ref[pl.ds((m * tile + r) * levels, levels), :] for r in range(tile)]
            for ref in (own_ref, near_ref, near_ref if far_ref is None else far_ref)
        )
        done = sweeps(with_halo(own, near, far, odd, low, high), rates, low_on, high_on, tile)
        for r in range(tile):
            rows = pl.ds(m * levels * tile + r, levels, stride=tile)
            out_ref[rows, :] = control_ref[rows, :] + done[r]


def end_kernel(members, tile, rates_ref, own_ref, near_ref, control_ref, out_ref, rows_ref, sem):
    _, low, high = edges()

    @pl.when(jnp.logical_not(low & high))
    def _():
        gradient_rows(members, tile, rates_ref, own_ref, near_ref, None, control_ref, rows_ref)
        copy = pltpu.make_async_copy(rows_ref, out_ref, sem)
        copy.start()
        copy.wait()


def inner_kernel(
    members, tile, rates_ref, own_ref, near_ref, far_ref, control_ref, _, out_ref, rows_ref, sem
):
    _, low, high = edges()

    @pl.when(low & high)
    def _():
        gradient_rows(
            members, tile, rates_ref, own_ref, near_ref, far_ref, control_ref, rows_ref
        )
        copy = pltpu.make_async_copy(rows_ref, out_ref, sem)
        copy.start()
        copy.wait()


def near_pairs(doms):
    return [(i, i ^ 1) for i in range(doms)]


def far_pairs(groups, doms):
    pairs = []
    for g in range(groups):
        for d in range(doms):
            if d in (0, doms - 1):
                pairs.append((g * doms + d, (g ^ 2) * doms + d))
            else:
                pairs.append((g * doms + d, g * doms + (d + 1 if d % 2 else d - 1)))
    return pairs


def core_order(groups, doms):
    return [
        [
            g * doms + 2 * chip + core
            for core in range(2)
            for g in GROUPS
            for chip in CHIPS
        ]
    ]


def beside(x, groups, doms):
    near = lax.ppermute(x, "dom", near_pairs(doms))
    far = lax.ppermute(x, ("grp", "dom"), far_pairs(groups, doms))
    return near, far


def small_device(pert_fcst, control, departures, obs_weight, diff_rate, step_counts):
    members, levels, variables = pert_fcst.shape[:3]
    tile, lons = control.shape[2], control.shape[3]
    groups, doms = lax.axis_size("grp"), lax.axis_size("dom")
    factor = 1.0 / math.sqrt(members * groups - 1)
    fields = members * levels * variables * tile
    flat = control.reshape(-1, lons)
    cells = pert_fcst.shape[-1]
    chosen = pl.pallas_call(
        functools.partial(choice_kernel, tile, lons // doms),
        out_shape=pltpu.VMEM((2 * lons // doms, 2 * cells // doms), jnp.bfloat16),
        out_specs=VMEM,
        cost_estimate=pl.CostEstimate(flops=10**10, bytes_accessed=0, transcendentals=0),
    )()
    tiles, rates = pl.pallas_call(
        functools.partial(pack_kernel, doms, tile, groups),
        out_shape=[
            jax.ShapeDtypeStruct((2, groups, doms // 2, lons // doms, fields), jnp.bfloat16),
            pltpu.VMEM((NSTEP, levels, lons), jnp.float32),
        ],
        in_specs=[VMEM, VMEM, ANY, ANY],
        out_specs=[ANY, VMEM],
        scratch_shapes=[
            pltpu.VMEM((2, doms // 2, lons // doms, fields), jnp.bfloat16),
            pltpu.VMEM((1, levels), jnp.float32),
            pltpu.VMEM((1, levels), jnp.int32),
            pltpu.SemaphoreType.DMA((groups + 2,)),
        ],
    )(
        in_vmem(chosen),
        in_vmem(pert_fcst.reshape(members * levels, variables, -1)),
        diff_rate.reshape(1, -1),
        step_counts.reshape(1, -1),
    )
    near, far = beside(flat, groups, doms)
    received = lax.all_to_all(
        tiles.reshape(-1, *tiles.shape[3:]),
        ("grp", "dom"),
        split_axis=0,
        concat_axis=0,
        tiled=True,
        axis_index_groups=core_order(groups, doms),
    )
    tiles = received.reshape(tiles.shape)
    local = pl.pallas_call(
        functools.partial(localize_kernel, members, tile),
        out_shape=pltpu.VMEM(flat.shape, jnp.float32),
        in_specs=[VMEM] * 4,
        out_specs=VMEM,
        cost_estimate=pl.CostEstimate(flops=10**10, bytes_accessed=0, transcendentals=0),
    )(in_vmem(rates), in_vmem(flat), in_vmem(near), in_vmem(far))
    locals_ = [local] + [
        lax.ppermute(local, "grp", [(i, i ^ j) for i in range(groups)]) for j in range(1, groups)
    ]
    increment, adjoint, for_far = pl.pallas_call(
        functools.partial(adjoint_kernel, members, levels, variables, tile, groups, factor),
        out_shape=[
            pltpu.VMEM((levels * variables * tile, lons), jnp.float32),
            pltpu.VMEM(flat.shape, jnp.float32),
            pltpu.VMEM((flat.shape[0] + levels, lons), jnp.float32),
        ],
        in_specs=[VMEM] * (groups + 3),
        out_specs=[VMEM, VMEM, VMEM],
    )(
        in_vmem(tiles),
        *[in_vmem(x) for x in locals_],
        in_vmem(obs_weight.reshape(-1, lons)),
        in_vmem(departures.reshape(-1, lons)),
    )
    near = lax.ppermute(adjoint, "dom", near_pairs(doms))
    far = lax.ppermute(for_far, ("grp", "dom"), far_pairs(groups, doms))
    at_ends = pl.pallas_call(
        functools.partial(end_kernel, members, tile),
        out_shape=jax.ShapeDtypeStruct(flat.shape, jnp.float32),
        in_specs=[VMEM] * 4,
        out_specs=ANY,
        scratch_shapes=[pltpu.VMEM(flat.shape, jnp.float32), pltpu.SemaphoreType.DMA],
        cost_estimate=pl.CostEstimate(flops=0, bytes_accessed=0, transcendentals=0),
    )(in_vmem(rates), in_vmem(adjoint), in_vmem(near), in_vmem(flat))
    gradient = pl.pallas_call(
        functools.partial(inner_kernel, members, tile),
        out_shape=jax.ShapeDtypeStruct(flat.shape, jnp.float32),
        in_specs=[VMEM] * 5 + [ANY],
        out_specs=ANY,
        scratch_shapes=[pltpu.VMEM(flat.shape, jnp.float32), pltpu.SemaphoreType.DMA],
        input_output_aliases={5: 0},
    )(in_vmem(rates), in_vmem(adjoint), in_vmem(near), in_vmem(far), in_vmem(flat), at_ends)
    return increment.reshape(departures.shape), gradient.reshape(control.shape)


def diffuse(field, diff_rate, step_counts):
    count, me = lax.axis_size("dom"), lax.axis_index("dom")
    forward = [(i, i + 1) for i in range(count - 1)]
    backward = [(target, source) for source, target in forward]
    tile = field.shape[2]
    low = lax.ppermute(field[:, :, tile - NSTEP :], "dom", forward)
    high = lax.ppermute(field[:, :, :NSTEP], "dom", backward)
    wide = jnp.concatenate([low, field, high], axis=2)
    row = lax.broadcasted_iota(jnp.int32, (1, 1, wide.shape[2], 1), 2)
    inside = ((row >= NSTEP) | (me > 0)) & ((row < NSTEP + tile) | (me < count - 1))
    for step in range(NSTEP):
        on = (step < step_counts)[None, :, None, None] & inside
        padded = jnp.pad(wide, ((0, 0), (0, 0), (1, 1), (0, 0)))
        laplace = (
            padded[:, :, 2:]
            + padded[:, :, :-2]
            + jnp.roll(wide, 1, axis=3)
            + jnp.roll(wide, -1, axis=3)
            - 4.0 * wide
        )
        wide = jnp.where(on, wide + diff_rate[None, :, None, None] * laplace, wide)
    return wide[:, :, NSTEP : NSTEP + tile]


def any_device(pert_fcst, control, departures, obs_weight, diff_rate, step_counts):
    members, levels, variables = pert_fcst.shape[:3]
    tile, lons = control.shape[2], control.shape[3]
    doms = lax.axis_size("dom")
    factor = 1.0 / math.sqrt(members * lax.axis_size("grp") - 1)
    localized = diffuse(control, diff_rate, step_counts)
    received = lax.all_to_all(
        pert_fcst.reshape(members * levels * variables, doms, -1),
        "dom",
        split_axis=1,
        concat_axis=1,
        tiled=True,
    )
    perturb = (
        received.reshape(-1, doms, tile, lons // doms)
        .transpose(0, 2, 1, 3)
        .reshape(members, levels, variables, tile, lons)
        .astype(jnp.float32)
    )
    increment = lax.psum(jnp.sum(perturb * localized[:, :, None], axis=0), "grp") * factor
    residual = obs_weight * (increment - departures)
    adjoint = jnp.sum(perturb * residual[None], axis=2) * factor
    return increment, control + diffuse(adjoint, diff_rate, step_counts)


def per_device(pert_fcst, control, departures, obs_weight, diff_rate, step_counts):
    members, levels, variables = pert_fcst.shape[:3]
    tile, lons = control.shape[2], control.shape[3]
    groups, doms = lax.axis_size("grp"), lax.axis_size("dom")
    small = (
        lons == 128
        and levels == 8
        and tile == NSTEP
        and members * levels * variables * tile == 128
        and doms == 2 * len(CHIPS)
        and lons // doms == 16
        and groups == len(GROUPS)
    )
    run = small_device if small else any_device
    return run(pert_fcst, control, departures, obs_weight, diff_rate, step_counts)


def solution(mesh):
    in_specs = (
        P("grp", None, None, "dom", None),
        P("grp", None, "dom", None),
        P(None, None, "dom", None),
        P(None, None, "dom", None),
        P(),
        P(),
    )
    out_specs = (P(None, None, "dom", None), P("grp", None, "dom", None))
    return jax.shard_map(
        per_device, mesh=mesh, in_specs=in_specs, out_specs=out_specs, check_vma=False
    )
```

```python
import functools
import math

import jax
import jax.numpy as jnp
from jax import lax
from jax.experimental import pallas as pl
from jax.experimental.pallas import tpu as pltpu
from jax.sharding import PartitionSpec as P

NSTEP = 4
CHIPS = (2, 3, 1, 0)
GROUPS = (3, 0, 1, 2)
VMEM = pl.BlockSpec(memory_space=pltpu.VMEM)
ANY = pl.BlockSpec(memory_space=pl.ANY)


def in_vmem(x):
    return pltpu.with_memory_space_constraint(x, pltpu.VMEM)


def down_rows(x, lons):
    wide = jnp.broadcast_to(x.astype(jnp.float32), (x.shape[1], x.shape[1]))
    on = lax.broadcasted_iota(jnp.int32, wide.shape, 0) == lax.broadcasted_iota(jnp.int32, wide.shape, 1)
    return jnp.broadcast_to(jnp.sum(jnp.where(on, wide, 0.0), axis=1, keepdims=True), (x.shape[1], lons))


def choice_kernel(rows, lons, out_ref):
    target = lax.broadcasted_iota(jnp.int32, out_ref.shape, 0)
    source = lax.broadcasted_iota(jnp.int32, out_ref.shape, 1)
    chosen = (target // lons == source // (rows * lons)) & (
        lax.rem(target, lons) == lax.rem(source, lons)
    )
    out_ref[...] = chosen.astype(jnp.float32).astype(jnp.bfloat16)


def pack_kernel(
    doms, rows, groups, chosen_ref, pert_ref, rate_ref, count_ref, out_ref, rates_ref, tiles_ref, rate_here, count_here, sems
):
    fetches = [
        pltpu.make_async_copy(rate_ref, rate_here, sems.at[groups]),
        pltpu.make_async_copy(count_ref, count_here, sems.at[groups + 1]),
    ]
    for copy in fetches:
        copy.start()
    _, variables, cells = pert_ref.shape
    lons = cells // (doms * rows)
    pert = pert_ref[...].astype(jnp.float32)
    fields = jnp.concatenate([pert[:, v, :] for v in range(variables)], axis=0)
    row_of = (lax.broadcasted_iota(jnp.int32, fields.shape, 1) // lons) % rows
    spread = jnp.concatenate(
        [jnp.where(row_of == r, fields, 0.0) for r in range(rows)], axis=0
    ).astype(jnp.bfloat16)
    chosen, pair = chosen_ref[...], chosen_ref.shape[1]
    for chip in range(doms // 2):
        both = lax.dot_general(
            chosen,
            spread[:, chip * pair : (chip + 1) * pair],
            (((1,), (1,)), ((), ())),
            preferred_element_type=jnp.float32,
        ).astype(jnp.bfloat16)
        for core in range(2):
            tiles_ref[core, CHIPS.index(chip)] = both[core * lons : (core + 1) * lons]
    stores = [pltpu.make_async_copy(tiles_ref, out_ref.at[:, g], sems.at[g]) for g in range(groups)]
    for copy in stores:
        copy.start()
    for copy in fetches:
        copy.wait()
    rate, count = (down_rows(ref[...], rates_ref.shape[2]) for ref in (rate_here, count_here))
    for step in range(NSTEP):
        rates_ref[step] = jnp.where(step < count, rate, 0.0)
    for copy in stores:
        copy.wait()


def sweeps(extended, rates, low_on, high_on, tile):
    lons = extended[0].shape[1]
    count = len(extended)
    powers = [list(extended)] + [[None] * count for _ in range(NSTEP)]
    for i in range(1, count - 1):
        deep = min(i, count - 1 - i, NSTEP)
        row = extended[i]
        pair = {
            k: pltpu.roll(row, k, 1) + pltpu.roll(row, lons - k, 1) for k in range(1, deep + 1)
        }
        pair[0] = row
        for n in range(1, deep + 1):
            total = pair[n]
            for k in range(1, (n + 1) // 2):
                total = total + float(math.comb(n, k)) * pair[n - 2 * k]
            if n % 2 == 0:
                total = total + float(math.comb(n, n // 2)) * row
            powers[n][i] = total
    for step in range(NSTEP):
        new = [[None] * count for _ in range(NSTEP - step)]
        for n in range(NSTEP - step):
            for i in range(step + 1 + n, count - 1 - step - n):
                if i < NSTEP:
                    rate = rates[step] * low_on
                elif i >= NSTEP + tile:
                    rate = rates[step] * high_on
                else:
                    rate = rates[step]
                mid = powers[n][i]
                laplace = powers[n][i + 1] + powers[n][i - 1] + powers[n + 1][i] - 4.0 * mid
                new[n][i] = mid + rate * laplace
        powers = new
    return powers[0][NSTEP : NSTEP + tile]


def edges():
    me, count = lax.axis_index("dom"), lax.axis_size("dom")
    odd = lax.rem(me, 2) == 1
    return odd, me > 0, me < count - 1


def with_halo(own, near, far, odd, low, high):
    below = [jnp.where(low, jnp.where(odd, n, f), 0.0) for n, f in zip(near, far)]
    above = [jnp.where(high, jnp.where(odd, f, n), 0.0) for n, f in zip(near, far)]
    return below + own + above


def localize_kernel(members, tile, rates_ref, own_ref, near_ref, far_ref, out_ref):
    levels = rates_ref.shape[1]
    odd, low, high = edges()
    low_on, high_on = low.astype(jnp.float32), high.astype(jnp.float32)
    rates = [rates_ref[step] for step in range(NSTEP)]
    for m in range(members):
        own, near, far = (
            [ref[pl.ds(m * levels * tile + r, levels, stride=tile), :] for r in range(tile)]
            for ref in (own_ref, near_ref, far_ref)
        )
        done = sweeps(with_halo(own, near, far, odd, low, high), rates, low_on, high_on, tile)
        for r in range(tile):
            out_ref[pl.ds((m * tile + r) * levels, levels), :] = done[r]


def adjoint_kernel(
    members, levels, variables, tile, groups, factor, tiles_ref, *refs
):
    local_refs, (weight_ref, depart_ref, inc_ref, adj_ref, far_ref) = refs[:groups], refs[groups:]
    mine = lax.axis_index("grp")
    sums, first = {}, None
    for j in range(groups):
        group = sum(
            jnp.where(jnp.bitwise_xor(mine, j) == g, GROUPS.index(g), 0) for g in range(groups)
        )
        blocks = [
            tiles_ref[core, group, CHIPS.index(chip)]
            for chip in range(len(CHIPS))
            for core in range(2)
        ]
        fields = jnp.concatenate(blocks, axis=0).T.astype(jnp.float32)
        if j == 0:
            first = fields
        for r in range(tile):
            for v in range(variables):
                for m in range(members):
                    at = ((r * variables + v) * members + m) * levels
                    term = (
                        fields[at : at + levels]
                        * local_refs[j][pl.ds((m * tile + r) * levels, levels), :]
                    )
                    sums[r, v] = sums[r, v] + term if (r, v) in sums else term
    for r in range(tile):
        residual = []
        for v in range(variables):
            rows = pl.ds(v * tile + r, levels, stride=variables * tile)
            increment = sums[r, v] * factor
            inc_ref[rows, :] = increment
            residual.append(weight_ref[rows, :] * (increment - depart_ref[rows, :]))
        for m in range(members):
            total = None
            for v in range(variables):
                at = ((r * variables + v) * members + m) * levels
                term = first[at : at + levels] * residual[v]
                total = term if total is None else total + term
            adj_ref[pl.ds((m * tile + r) * levels, levels), :] = total * factor
            far_ref[pl.ds((m * tile + r) * levels, levels), :] = total * factor
    far_ref[pl.ds(members * tile * levels, levels), :] = jnp.zeros((levels, inc_ref.shape[1]), jnp.float32)


def gradient_rows(members, tile, rates_ref, own_ref, near_ref, far_ref, control_ref, out_ref):
    levels = rates_ref.shape[1]
    odd, low, high = edges()
    low_on, high_on = low.astype(jnp.float32), high.astype(jnp.float32)
    rates = [rates_ref[step] for step in range(NSTEP)]
    for m in range(members):
        own, near, far = (
            [ref[pl.ds((m * tile + r) * levels, levels), :] for r in range(tile)]
            for ref in (own_ref, near_ref, near_ref if far_ref is None else far_ref)
        )
        done = sweeps(with_halo(own, near, far, odd, low, high), rates, low_on, high_on, tile)
        for r in range(tile):
            rows = pl.ds(m * levels * tile + r, levels, stride=tile)
            out_ref[rows, :] = control_ref[rows, :] + done[r]


def end_kernel(members, tile, rates_ref, own_ref, near_ref, control_ref, out_ref, rows_ref, sem):
    _, low, high = edges()

    @pl.when(jnp.logical_not(low & high))
    def _():
        gradient_rows(members, tile, rates_ref, own_ref, near_ref, None, control_ref, rows_ref)
        copy = pltpu.make_async_copy(rows_ref, out_ref, sem)
        copy.start()
        copy.wait()


def inner_kernel(
    members, tile, rates_ref, own_ref, near_ref, far_ref, control_ref, _, out_ref, rows_ref, sem
):
    _, low, high = edges()

    @pl.when(low & high)
    def _():
        gradient_rows(
            members, tile, rates_ref, own_ref, near_ref, far_ref, control_ref, rows_ref
        )
        copy = pltpu.make_async_copy(rows_ref, out_ref, sem)
        copy.start()
        copy.wait()


def near_pairs(doms):
    return [(i, i ^ 1) for i in range(doms)]


def far_pairs(groups, doms):
    pairs = []
    for g in range(groups):
        for d in range(doms):
            if d in (0, doms - 1):
                pairs.append((g * doms + d, (g ^ 1) * doms + d))
            else:
                pairs.append((g * doms + d, g * doms + (d + 1 if d % 2 else d - 1)))
    return pairs


def core_order(groups, doms):
    return [
        [
            g * doms + 2 * chip + core
            for core in range(2)
            for g in GROUPS
            for chip in CHIPS
        ]
    ]


def beside(x, groups, doms):
    near = lax.ppermute(x, "dom", near_pairs(doms))
    far = lax.ppermute(x, ("grp", "dom"), far_pairs(groups, doms))
    return near, far


def small_device(pert_fcst, control, departures, obs_weight, diff_rate, step_counts):
    members, levels, variables = pert_fcst.shape[:3]
    tile, lons = control.shape[2], control.shape[3]
    groups, doms = lax.axis_size("grp"), lax.axis_size("dom")
    factor = 1.0 / math.sqrt(members * groups - 1)
    fields = members * levels * variables * tile
    flat = control.reshape(-1, lons)
    cells = pert_fcst.shape[-1]
    chosen = pl.pallas_call(
        functools.partial(choice_kernel, tile, lons // doms),
        out_shape=pltpu.VMEM((2 * lons // doms, 2 * cells // doms), jnp.bfloat16),
        out_specs=VMEM,
        cost_estimate=pl.CostEstimate(flops=10**10, bytes_accessed=0, transcendentals=0),
    )()
    tiles, rates = pl.pallas_call(
        functools.partial(pack_kernel, doms, tile, groups),
        out_shape=[
            jax.ShapeDtypeStruct((2, groups, doms // 2, lons // doms, fields), jnp.bfloat16),
            pltpu.VMEM((NSTEP, levels, lons), jnp.float32),
        ],
        in_specs=[VMEM, VMEM, ANY, ANY],
        out_specs=[ANY, VMEM],
        scratch_shapes=[
            pltpu.VMEM((2, doms // 2, lons // doms, fields), jnp.bfloat16),
            pltpu.VMEM((1, levels), jnp.float32),
            pltpu.VMEM((1, levels), jnp.int32),
            pltpu.SemaphoreType.DMA((groups + 2,)),
        ],
    )(
        in_vmem(chosen),
        in_vmem(pert_fcst.reshape(members * levels, variables, -1)),
        diff_rate.reshape(1, -1),
        step_counts.reshape(1, -1),
    )
    near, far = beside(flat, groups, doms)
    received = lax.all_to_all(
        tiles.reshape(-1, *tiles.shape[3:]),
        ("grp", "dom"),
        split_axis=0,
        concat_axis=0,
        tiled=True,
        axis_index_groups=core_order(groups, doms),
    )
    tiles = received.reshape(tiles.shape)
    local = pl.pallas_call(
        functools.partial(localize_kernel, members, tile),
        out_shape=pltpu.VMEM(flat.shape, jnp.float32),
        in_specs=[VMEM] * 4,
        out_specs=VMEM,
        cost_estimate=pl.CostEstimate(flops=10**10, bytes_accessed=0, transcendentals=0),
    )(in_vmem(rates), in_vmem(flat), in_vmem(near), in_vmem(far))
    locals_ = [local] + [
        lax.ppermute(local, "grp", [(i, i ^ j) for i in range(groups)]) for j in range(1, groups)
    ]
    increment, adjoint, for_far = pl.pallas_call(
        functools.partial(adjoint_kernel, members, levels, variables, tile, groups, factor),
        out_shape=[
            pltpu.VMEM((levels * variables * tile, lons), jnp.float32),
            pltpu.VMEM(flat.shape, jnp.float32),
            pltpu.VMEM((flat.shape[0] + levels, lons), jnp.float32),
        ],
        in_specs=[VMEM] * (groups + 3),
        out_specs=[VMEM, VMEM, VMEM],
    )(
        in_vmem(tiles),
        *[in_vmem(x) for x in locals_],
        in_vmem(obs_weight.reshape(-1, lons)),
        in_vmem(departures.reshape(-1, lons)),
    )
    near = lax.ppermute(adjoint, "dom", near_pairs(doms))
    far = lax.ppermute(for_far, ("grp", "dom"), far_pairs(groups, doms))
    at_ends = pl.pallas_call(
        functools.partial(end_kernel, members, tile),
        out_shape=jax.ShapeDtypeStruct(flat.shape, jnp.float32),
        in_specs=[VMEM] * 4,
        out_specs=ANY,
        scratch_shapes=[pltpu.VMEM(flat.shape, jnp.float32), pltpu.SemaphoreType.DMA],
        cost_estimate=pl.CostEstimate(flops=0, bytes_accessed=0, transcendentals=0),
    )(in_vmem(rates), in_vmem(adjoint), in_vmem(near), in_vmem(flat))
    gradient = pl.pallas_call(
        functools.partial(inner_kernel, members, tile),
        out_shape=jax.ShapeDtypeStruct(flat.shape, jnp.float32),
        in_specs=[VMEM] * 5 + [ANY],
        out_specs=ANY,
        scratch_shapes=[pltpu.VMEM(flat.shape, jnp.float32), pltpu.SemaphoreType.DMA],
        input_output_aliases={5: 0},
    )(in_vmem(rates), in_vmem(adjoint), in_vmem(near), in_vmem(far), in_vmem(flat), at_ends)
    return increment.reshape(departures.shape), gradient.reshape(control.shape)


def diffuse(field, diff_rate, step_counts):
    count, me = lax.axis_size("dom"), lax.axis_index("dom")
    forward = [(i, i + 1) for i in range(count - 1)]
    backward = [(target, source) for source, target in forward]
    tile = field.shape[2]
    low = lax.ppermute(field[:, :, tile - NSTEP :], "dom", forward)
    high = lax.ppermute(field[:, :, :NSTEP], "dom", backward)
    wide = jnp.concatenate([low, field, high], axis=2)
    row = lax.broadcasted_iota(jnp.int32, (1, 1, wide.shape[2], 1), 2)
    inside = ((row >= NSTEP) | (me > 0)) & ((row < NSTEP + tile) | (me < count - 1))
    for step in range(NSTEP):
        on = (step < step_counts)[None, :, None, None] & inside
        padded = jnp.pad(wide, ((0, 0), (0, 0), (1, 1), (0, 0)))
        laplace = (
            padded[:, :, 2:]
            + padded[:, :, :-2]
            + jnp.roll(wide, 1, axis=3)
            + jnp.roll(wide, -1, axis=3)
            - 4.0 * wide
        )
        wide = jnp.where(on, wide + diff_rate[None, :, None, None] * laplace, wide)
    return wide[:, :, NSTEP : NSTEP + tile]


def any_device(pert_fcst, control, departures, obs_weight, diff_rate, step_counts):
    members, levels, variables = pert_fcst.shape[:3]
    tile, lons = control.shape[2], control.shape[3]
    doms = lax.axis_size("dom")
    factor = 1.0 / math.sqrt(members * lax.axis_size("grp") - 1)
    localized = diffuse(control, diff_rate, step_counts)
    received = lax.all_to_all(
        pert_fcst.reshape(members * levels * variables, doms, -1),
        "dom",
        split_axis=1,
        concat_axis=1,
        tiled=True,
    )
    perturb = (
        received.reshape(-1, doms, tile, lons // doms)
        .transpose(0, 2, 1, 3)
        .reshape(members, levels, variables, tile, lons)
        .astype(jnp.float32)
    )
    increment = lax.psum(jnp.sum(perturb * localized[:, :, None], axis=0), "grp") * factor
    residual = obs_weight * (increment - departures)
    adjoint = jnp.sum(perturb * residual[None], axis=2) * factor
    return increment, control + diffuse(adjoint, diff_rate, step_counts)


def per_device(pert_fcst, control, departures, obs_weight, diff_rate, step_counts):
    members, levels, variables = pert_fcst.shape[:3]
    tile, lons = control.shape[2], control.shape[3]
    groups, doms = lax.axis_size("grp"), lax.axis_size("dom")
    small = (
        lons == 128
        and levels == 8
        and tile == NSTEP
        and members * levels * variables * tile == 128
        and doms == 2 * len(CHIPS)
        and lons // doms == 16
        and groups == len(GROUPS)
    )
    run = small_device if small else any_device
    return run(pert_fcst, control, departures, obs_weight, diff_rate, step_counts)


def solution(mesh):
    in_specs = (
        P("grp", None, None, "dom", None),
        P("grp", None, "dom", None),
        P(None, None, "dom", None),
        P(None, None, "dom", None),
        P(),
        P(),
    )
    out_specs = (P(None, None, "dom", None), P("grp", None, "dom", None))
    return jax.shard_map(
        per_device, mesh=mesh, in_specs=in_specs, out_specs=out_specs, check_vma=False
    )
```

```python
import functools
import math

import jax
import jax.numpy as jnp
from jax import lax
from jax.experimental import pallas as pl
from jax.experimental.pallas import tpu as pltpu
from jax.sharding import PartitionSpec as P

NSTEP = 4
CHIPS = (2, 3, 1, 0)
GROUPS = (3, 0, 1, 2)
VMEM = pl.BlockSpec(memory_space=pltpu.VMEM)
ANY = pl.BlockSpec(memory_space=pl.ANY)


def in_vmem(x):
    return pltpu.with_memory_space_constraint(x, pltpu.VMEM)


def down_rows(x, lons):
    wide = jnp.broadcast_to(x.astype(jnp.float32), (x.shape[1], x.shape[1]))
    on = lax.broadcasted_iota(jnp.int32, wide.shape, 0) == lax.broadcasted_iota(jnp.int32, wide.shape, 1)
    return jnp.broadcast_to(jnp.sum(jnp.where(on, wide, 0.0), axis=1, keepdims=True), (x.shape[1], lons))


def choice_kernel(rows, lons, out_ref):
    target = lax.broadcasted_iota(jnp.int32, out_ref.shape, 0)
    source = lax.broadcasted_iota(jnp.int32, out_ref.shape, 1)
    chosen = (target // lons == source // (rows * lons)) & (
        lax.rem(target, lons) == lax.rem(source, lons)
    )
    out_ref[...] = chosen.astype(jnp.float32).astype(jnp.bfloat16)


def pack_kernel(
    doms, rows, groups, chosen_ref, pert_ref, rate_ref, count_ref, out_ref, rates_ref, tiles_ref, rate_here, count_here, sems
):
    fetches = [
        pltpu.make_async_copy(rate_ref, rate_here, sems.at[1]),
        pltpu.make_async_copy(count_ref, count_here, sems.at[2]),
    ]
    for copy in fetches:
        copy.start()
    _, variables, cells = pert_ref.shape
    lons = cells // (doms * rows)
    pert = pert_ref[...].astype(jnp.float32)
    fields = jnp.concatenate([pert[:, v, :] for v in range(variables)], axis=0)
    row_of = (lax.broadcasted_iota(jnp.int32, fields.shape, 1) // lons) % rows
    spread = jnp.concatenate(
        [jnp.where(row_of == r, fields, 0.0) for r in range(rows)], axis=0
    ).astype(jnp.bfloat16)
    chosen, pair = chosen_ref[...], chosen_ref.shape[1]
    for chip in range(doms // 2):
        both = lax.dot_general(
            chosen,
            spread[:, chip * pair : (chip + 1) * pair],
            (((1,), (1,)), ((), ())),
            preferred_element_type=jnp.float32,
        ).astype(jnp.bfloat16)
        for core in range(2):
            for g in range(groups):
                tiles_ref[core, g, CHIPS.index(chip)] = both[core * lons : (core + 1) * lons]
    stores = [pltpu.make_async_copy(tiles_ref, out_ref, sems.at[0])]
    for copy in stores:
        copy.start()
    for copy in fetches:
        copy.wait()
    rate, count = (down_rows(ref[...], rates_ref.shape[2]) for ref in (rate_here, count_here))
    for step in range(NSTEP):
        rates_ref[step] = jnp.where(step < count, rate, 0.0)
    for copy in stores:
        copy.wait()


def sweeps(extended, rates, low_on, high_on, tile):
    lons = extended[0].shape[1]
    count = len(extended)
    powers = [list(extended)] + [[None] * count for _ in range(NSTEP)]
    for i in range(1, count - 1):
        deep = min(i, count - 1 - i, NSTEP)
        row = extended[i]
        pair = {
            k: pltpu.roll(row, k, 1) + pltpu.roll(row, lons - k, 1) for k in range(1, deep + 1)
        }
        pair[0] = row
        for n in range(1, deep + 1):
            total = pair[n]
            for k in range(1, (n + 1) // 2):
                total = total + float(math.comb(n, k)) * pair[n - 2 * k]
            if n % 2 == 0:
                total = total + float(math.comb(n, n // 2)) * row
            powers[n][i] = total
    for step in range(NSTEP):
        new = [[None] * count for _ in range(NSTEP - step)]
        for n in range(NSTEP - step):
            for i in range(step + 1 + n, count - 1 - step - n):
                if i < NSTEP:
                    rate = rates[step] * low_on
                elif i >= NSTEP + tile:
                    rate = rates[step] * high_on
                else:
                    rate = rates[step]
                mid = powers[n][i]
                laplace = powers[n][i + 1] + powers[n][i - 1] + powers[n + 1][i] - 4.0 * mid
                new[n][i] = mid + rate * laplace
        powers = new
    return powers[0][NSTEP : NSTEP + tile]


def edges():
    me, count = lax.axis_index("dom"), lax.axis_size("dom")
    odd = lax.rem(me, 2) == 1
    return odd, me > 0, me < count - 1


def with_halo(own, near, far, odd, low, high):
    below = [jnp.where(low, jnp.where(odd, n, f), 0.0) for n, f in zip(near, far)]
    above = [jnp.where(high, jnp.where(odd, f, n), 0.0) for n, f in zip(near, far)]
    return below + own + above


def localize_kernel(members, tile, rates_ref, own_ref, near_ref, far_ref, out_ref):
    levels = rates_ref.shape[1]
    odd, low, high = edges()
    low_on, high_on = low.astype(jnp.float32), high.astype(jnp.float32)
    rates = [rates_ref[step] for step in range(NSTEP)]
    for m in range(members):
        own, near, far = (
            [ref[pl.ds(m * levels * tile + r, levels, stride=tile), :] for r in range(tile)]
            for ref in (own_ref, near_ref, far_ref)
        )
        done = sweeps(with_halo(own, near, far, odd, low, high), rates, low_on, high_on, tile)
        for r in range(tile):
            out_ref[pl.ds((m * tile + r) * levels, levels), :] = done[r]


def adjoint_kernel(
    members, levels, variables, tile, groups, factor, tiles_ref, *refs
):
    local_refs, (weight_ref, depart_ref, inc_ref, adj_ref, far_ref) = refs[:groups], refs[groups:]
    mine = lax.axis_index("grp")
    sums, first = {}, None
    for j in range(groups):
        group = sum(
            jnp.where(jnp.bitwise_xor(mine, j) == g, GROUPS.index(g), 0) for g in range(groups)
        )
        blocks = [
            tiles_ref[core, group, CHIPS.index(chip)]
            for chip in range(len(CHIPS))
            for core in range(2)
        ]
        fields = jnp.concatenate(blocks, axis=0).T.astype(jnp.float32)
        if j == 0:
            first = fields
        for r in range(tile):
            for v in range(variables):
                for m in range(members):
                    at = ((r * variables + v) * members + m) * levels
                    term = (
                        fields[at : at + levels]
                        * local_refs[j][pl.ds((m * tile + r) * levels, levels), :]
                    )
                    sums[r, v] = sums[r, v] + term if (r, v) in sums else term
    for r in range(tile):
        residual = []
        for v in range(variables):
            rows = pl.ds(v * tile + r, levels, stride=variables * tile)
            increment = sums[r, v] * factor
            inc_ref[rows, :] = increment
            residual.append(weight_ref[rows, :] * (increment - depart_ref[rows, :]))
        for m in range(members):
            total = None
            for v in range(variables):
                at = ((r * variables + v) * members + m) * levels
                term = first[at : at + levels] * residual[v]
                total = term if total is None else total + term
            adj_ref[pl.ds((m * tile + r) * levels, levels), :] = total * factor
            far_ref[pl.ds((m * tile + r) * levels, levels), :] = total * factor
    far_ref[pl.ds(members * tile * levels, levels), :] = jnp.zeros((levels, inc_ref.shape[1]), jnp.float32)


def gradient_rows(members, tile, rates_ref, own_ref, near_ref, far_ref, control_ref, out_ref):
    levels = rates_ref.shape[1]
    odd, low, high = edges()
    low_on, high_on = low.astype(jnp.float32), high.astype(jnp.float32)
    rates = [rates_ref[step] for step in range(NSTEP)]
    for m in range(members):
        own, near, far = (
            [ref[pl.ds((m * tile + r) * levels, levels), :] for r in range(tile)]
            for ref in (own_ref, near_ref, near_ref if far_ref is None else far_ref)
        )
        done = sweeps(with_halo(own, near, far, odd, low, high), rates, low_on, high_on, tile)
        for r in range(tile):
            rows = pl.ds(m * levels * tile + r, levels, stride=tile)
            out_ref[rows, :] = control_ref[rows, :] + done[r]


def end_kernel(members, tile, rates_ref, own_ref, near_ref, control_ref, out_ref, rows_ref, sem):
    _, low, high = edges()

    @pl.when(jnp.logical_not(low & high))
    def _():
        gradient_rows(members, tile, rates_ref, own_ref, near_ref, None, control_ref, rows_ref)
        copy = pltpu.make_async_copy(rows_ref, out_ref, sem)
        copy.start()
        copy.wait()


def inner_kernel(
    members, tile, rates_ref, own_ref, near_ref, far_ref, control_ref, _, out_ref, rows_ref, sem
):
    _, low, high = edges()

    @pl.when(low & high)
    def _():
        gradient_rows(
            members, tile, rates_ref, own_ref, near_ref, far_ref, control_ref, rows_ref
        )
        copy = pltpu.make_async_copy(rows_ref, out_ref, sem)
        copy.start()
        copy.wait()


def near_pairs(doms):
    return [(i, i ^ 1) for i in range(doms)]


def far_pairs(groups, doms):
    pairs = []
    for g in range(groups):
        for d in range(doms):
            if d in (0, doms - 1):
                pairs.append((g * doms + d, (g ^ 1) * doms + d))
            else:
                pairs.append((g * doms + d, g * doms + (d + 1 if d % 2 else d - 1)))
    return pairs


def core_order(groups, doms):
    return [
        [
            g * doms + 2 * chip + core
            for core in range(2)
            for g in GROUPS
            for chip in CHIPS
        ]
    ]


def beside(x, groups, doms):
    near = lax.ppermute(x, "dom", near_pairs(doms))
    far = lax.ppermute(x, ("grp", "dom"), far_pairs(groups, doms))
    return near, far


def small_device(pert_fcst, control, departures, obs_weight, diff_rate, step_counts):
    members, levels, variables = pert_fcst.shape[:3]
    tile, lons = control.shape[2], control.shape[3]
    groups, doms = lax.axis_size("grp"), lax.axis_size("dom")
    factor = 1.0 / math.sqrt(members * groups - 1)
    fields = members * levels * variables * tile
    flat = control.reshape(-1, lons)
    cells = pert_fcst.shape[-1]
    chosen = pl.pallas_call(
        functools.partial(choice_kernel, tile, lons // doms),
        out_shape=pltpu.VMEM((2 * lons // doms, 2 * cells // doms), jnp.bfloat16),
        out_specs=VMEM,
        cost_estimate=pl.CostEstimate(flops=10**10, bytes_accessed=0, transcendentals=0),
    )()
    tiles, rates = pl.pallas_call(
        functools.partial(pack_kernel, doms, tile, groups),
        out_shape=[
            jax.ShapeDtypeStruct((2, groups, doms // 2, lons // doms, fields), jnp.bfloat16),
            pltpu.VMEM((NSTEP, levels, lons), jnp.float32),
        ],
        in_specs=[VMEM, VMEM, ANY, ANY],
        out_specs=[ANY, VMEM],
        scratch_shapes=[
            pltpu.VMEM((2, groups, doms // 2, lons // doms, fields), jnp.bfloat16),
            pltpu.VMEM((1, levels), jnp.float32),
            pltpu.VMEM((1, levels), jnp.int32),
            pltpu.SemaphoreType.DMA((3,)),
        ],
    )(
        in_vmem(chosen),
        in_vmem(pert_fcst.reshape(members * levels, variables, -1)),
        diff_rate.reshape(1, -1),
        step_counts.reshape(1, -1),
    )
    near, far = beside(flat, groups, doms)
    received = lax.all_to_all(
        tiles.reshape(-1, *tiles.shape[3:]),
        ("grp", "dom"),
        split_axis=0,
        concat_axis=0,
        tiled=True,
        axis_index_groups=core_order(groups, doms),
    )
    tiles = received.reshape(tiles.shape)
    local = pl.pallas_call(
        functools.partial(localize_kernel, members, tile),
        out_shape=pltpu.VMEM(flat.shape, jnp.float32),
        in_specs=[VMEM] * 4,
        out_specs=VMEM,
        cost_estimate=pl.CostEstimate(flops=10**10, bytes_accessed=0, transcendentals=0),
    )(in_vmem(rates), in_vmem(flat), in_vmem(near), in_vmem(far))
    locals_ = [local] + [
        lax.ppermute(local, "grp", [(i, i ^ j) for i in range(groups)]) for j in range(1, groups)
    ]
    increment, adjoint, for_far = pl.pallas_call(
        functools.partial(adjoint_kernel, members, levels, variables, tile, groups, factor),
        out_shape=[
            pltpu.VMEM((levels * variables * tile, lons), jnp.float32),
            pltpu.VMEM(flat.shape, jnp.float32),
            pltpu.VMEM((flat.shape[0] + levels, lons), jnp.float32),
        ],
        in_specs=[VMEM] * (groups + 3),
        out_specs=[VMEM, VMEM, VMEM],
    )(
        in_vmem(tiles),
        *[in_vmem(x) for x in locals_],
        in_vmem(obs_weight.reshape(-1, lons)),
        in_vmem(departures.reshape(-1, lons)),
    )
    near = lax.ppermute(adjoint, "dom", near_pairs(doms))
    far = lax.ppermute(for_far, ("grp", "dom"), far_pairs(groups, doms))
    at_ends = pl.pallas_call(
        functools.partial(end_kernel, members, tile),
        out_shape=jax.ShapeDtypeStruct(flat.shape, jnp.float32),
        in_specs=[VMEM] * 4,
        out_specs=ANY,
        scratch_shapes=[pltpu.VMEM(flat.shape, jnp.float32), pltpu.SemaphoreType.DMA],
        cost_estimate=pl.CostEstimate(flops=0, bytes_accessed=0, transcendentals=0),
    )(in_vmem(rates), in_vmem(adjoint), in_vmem(near), in_vmem(flat))
    gradient = pl.pallas_call(
        functools.partial(inner_kernel, members, tile),
        out_shape=jax.ShapeDtypeStruct(flat.shape, jnp.float32),
        in_specs=[VMEM] * 5 + [ANY],
        out_specs=ANY,
        scratch_shapes=[pltpu.VMEM(flat.shape, jnp.float32), pltpu.SemaphoreType.DMA],
        input_output_aliases={5: 0},
    )(in_vmem(rates), in_vmem(adjoint), in_vmem(near), in_vmem(far), in_vmem(flat), at_ends)
    return increment.reshape(departures.shape), gradient.reshape(control.shape)


def diffuse(field, diff_rate, step_counts):
    count, me = lax.axis_size("dom"), lax.axis_index("dom")
    forward = [(i, i + 1) for i in range(count - 1)]
    backward = [(target, source) for source, target in forward]
    tile = field.shape[2]
    low = lax.ppermute(field[:, :, tile - NSTEP :], "dom", forward)
    high = lax.ppermute(field[:, :, :NSTEP], "dom", backward)
    wide = jnp.concatenate([low, field, high], axis=2)
    row = lax.broadcasted_iota(jnp.int32, (1, 1, wide.shape[2], 1), 2)
    inside = ((row >= NSTEP) | (me > 0)) & ((row < NSTEP + tile) | (me < count - 1))
    for step in range(NSTEP):
        on = (step < step_counts)[None, :, None, None] & inside
        padded = jnp.pad(wide, ((0, 0), (0, 0), (1, 1), (0, 0)))
        laplace = (
            padded[:, :, 2:]
            + padded[:, :, :-2]
            + jnp.roll(wide, 1, axis=3)
            + jnp.roll(wide, -1, axis=3)
            - 4.0 * wide
        )
        wide = jnp.where(on, wide + diff_rate[None, :, None, None] * laplace, wide)
    return wide[:, :, NSTEP : NSTEP + tile]


def any_device(pert_fcst, control, departures, obs_weight, diff_rate, step_counts):
    members, levels, variables = pert_fcst.shape[:3]
    tile, lons = control.shape[2], control.shape[3]
    doms = lax.axis_size("dom")
    factor = 1.0 / math.sqrt(members * lax.axis_size("grp") - 1)
    localized = diffuse(control, diff_rate, step_counts)
    received = lax.all_to_all(
        pert_fcst.reshape(members * levels * variables, doms, -1),
        "dom",
        split_axis=1,
        concat_axis=1,
        tiled=True,
    )
    perturb = (
        received.reshape(-1, doms, tile, lons // doms)
        .transpose(0, 2, 1, 3)
        .reshape(members, levels, variables, tile, lons)
        .astype(jnp.float32)
    )
    increment = lax.psum(jnp.sum(perturb * localized[:, :, None], axis=0), "grp") * factor
    residual = obs_weight * (increment - departures)
    adjoint = jnp.sum(perturb * residual[None], axis=2) * factor
    return increment, control + diffuse(adjoint, diff_rate, step_counts)


def per_device(pert_fcst, control, departures, obs_weight, diff_rate, step_counts):
    members, levels, variables = pert_fcst.shape[:3]
    tile, lons = control.shape[2], control.shape[3]
    groups, doms = lax.axis_size("grp"), lax.axis_size("dom")
    small = (
        lons == 128
        and levels == 8
        and tile == NSTEP
        and members * levels * variables * tile == 128
        and doms == 2 * len(CHIPS)
        and lons // doms == 16
        and groups == len(GROUPS)
    )
    run = small_device if small else any_device
    return run(pert_fcst, control, departures, obs_weight, diff_rate, step_counts)


def solution(mesh):
    in_specs = (
        P("grp", None, None, "dom", None),
        P("grp", None, "dom", None),
        P(None, None, "dom", None),
        P(None, None, "dom", None),
        P(),
        P(),
    )
    out_specs = (P(None, None, "dom", None), P("grp", None, "dom", None))
    return jax.shard_map(
        per_device, mesh=mesh, in_specs=in_specs, out_specs=out_specs, check_vma=False
    )
```

```python
import functools
import math

import jax
import jax.numpy as jnp
from jax import lax
from jax.experimental import pallas as pl
from jax.experimental.pallas import tpu as pltpu
from jax.sharding import PartitionSpec as P

NSTEP = 4
CHIPS = (2, 3, 1, 0)
GROUPS = (3, 0, 1, 2)
VMEM = pl.BlockSpec(memory_space=pltpu.VMEM)
ANY = pl.BlockSpec(memory_space=pl.ANY)


def in_vmem(x):
    return pltpu.with_memory_space_constraint(x, pltpu.VMEM)


def down_rows(x, lons):
    wide = jnp.broadcast_to(x.astype(jnp.float32), (x.shape[1], x.shape[1]))
    on = lax.broadcasted_iota(jnp.int32, wide.shape, 0) == lax.broadcasted_iota(jnp.int32, wide.shape, 1)
    return jnp.broadcast_to(jnp.sum(jnp.where(on, wide, 0.0), axis=1, keepdims=True), (x.shape[1], lons))


def choice_kernel(rows, lons, out_ref):
    target = lax.broadcasted_iota(jnp.int32, out_ref.shape, 0)
    source = lax.broadcasted_iota(jnp.int32, out_ref.shape, 1)
    chosen = (target // lons == source // (rows * lons)) & (
        lax.rem(target, lons) == lax.rem(source, lons)
    )
    out_ref[...] = chosen.astype(jnp.float32).astype(jnp.bfloat16)


def pack_kernel(
    doms, rows, groups, chosen_ref, pert_ref, rate_ref, count_ref, out_ref, rates_ref, tiles_ref, rate_here, count_here, sems
):
    fetches = [
        pltpu.make_async_copy(rate_ref, rate_here, sems.at[groups]),
        pltpu.make_async_copy(count_ref, count_here, sems.at[groups + 1]),
    ]
    for copy in fetches:
        copy.start()
    _, variables, cells = pert_ref.shape
    lons = cells // (doms * rows)
    pert = pert_ref[...].astype(jnp.float32)
    fields = jnp.concatenate([pert[:, v, :] for v in range(variables)], axis=0)
    fields = fields.astype(jnp.bfloat16)
    row_of = (lax.broadcasted_iota(jnp.int32, fields.shape, 1) // lons) % rows
    spread = jnp.concatenate(
        [jnp.where(row_of == r, fields, jnp.bfloat16(0)) for r in range(rows)], axis=0
    )
    chosen, pair = chosen_ref[...], chosen_ref.shape[1]
    for chip in range(doms // 2):
        both = lax.dot_general(
            chosen,
            spread[:, chip * pair : (chip + 1) * pair],
            (((1,), (1,)), ((), ())),
            preferred_element_type=jnp.float32,
        ).astype(jnp.bfloat16)
        for core in range(2):
            tiles_ref[core, CHIPS.index(chip)] = both[core * lons : (core + 1) * lons]
    stores = [pltpu.make_async_copy(tiles_ref, out_ref.at[:, g], sems.at[g]) for g in range(groups)]
    for copy in stores:
        copy.start()
    for copy in fetches:
        copy.wait()
    rate, count = (down_rows(ref[...], rates_ref.shape[2]) for ref in (rate_here, count_here))
    for step in range(NSTEP):
        rates_ref[step] = jnp.where(step < count, rate, 0.0)
    for copy in stores:
        copy.wait()


def sweeps(extended, rates, low_on, high_on, tile):
    lons = extended[0].shape[1]
    count = len(extended)
    powers = [list(extended)] + [[None] * count for _ in range(NSTEP)]
    for i in range(1, count - 1):
        deep = min(i, count - 1 - i, NSTEP)
        row = extended[i]
        pair = {
            k: pltpu.roll(row, k, 1) + pltpu.roll(row, lons - k, 1) for k in range(1, deep + 1)
        }
        pair[0] = row
        for n in range(1, deep + 1):
            total = pair[n]
            for k in range(1, (n + 1) // 2):
                total = total + float(math.comb(n, k)) * pair[n - 2 * k]
            if n % 2 == 0:
                total = total + float(math.comb(n, n // 2)) * row
            powers[n][i] = total
    for step in range(NSTEP):
        new = [[None] * count for _ in range(NSTEP - step)]
        for n in range(NSTEP - step):
            for i in range(step + 1 + n, count - 1 - step - n):
                if i < NSTEP:
                    rate = rates[step] * low_on
                elif i >= NSTEP + tile:
                    rate = rates[step] * high_on
                else:
                    rate = rates[step]
                mid = powers[n][i]
                laplace = powers[n][i + 1] + powers[n][i - 1] + powers[n + 1][i] - 4.0 * mid
                new[n][i] = mid + rate * laplace
        powers = new
    return powers[0][NSTEP : NSTEP + tile]


def edges():
    me, count = lax.axis_index("dom"), lax.axis_size("dom")
    odd = lax.rem(me, 2) == 1
    return odd, me > 0, me < count - 1


def with_halo(own, near, far, odd, low, high):
    below = [jnp.where(low, jnp.where(odd, n, f), 0.0) for n, f in zip(near, far)]
    above = [jnp.where(high, jnp.where(odd, f, n), 0.0) for n, f in zip(near, far)]
    return below + own + above


def localize_kernel(members, tile, rates_ref, own_ref, near_ref, far_ref, out_ref):
    levels = rates_ref.shape[1]
    odd, low, high = edges()
    low_on, high_on = low.astype(jnp.float32), high.astype(jnp.float32)
    rates = [rates_ref[step] for step in range(NSTEP)]
    for m in range(members):
        own, near, far = (
            [ref[pl.ds(m * levels * tile + r, levels, stride=tile), :] for r in range(tile)]
            for ref in (own_ref, near_ref, far_ref)
        )
        done = sweeps(with_halo(own, near, far, odd, low, high), rates, low_on, high_on, tile)
        for r in range(tile):
            out_ref[pl.ds((m * tile + r) * levels, levels), :] = done[r]


def adjoint_kernel(
    members, levels, variables, tile, groups, factor, tiles_ref, *refs
):
    local_refs, (weight_ref, depart_ref, inc_ref, adj_ref, far_ref) = refs[:groups], refs[groups:]
    mine = lax.axis_index("grp")
    sums, first = {}, None
    for j in range(groups):
        group = sum(
            jnp.where(jnp.bitwise_xor(mine, j) == g, GROUPS.index(g), 0) for g in range(groups)
        )
        blocks = [
            tiles_ref[core, group, CHIPS.index(chip)]
            for chip in range(len(CHIPS))
            for core in range(2)
        ]
        fields = jnp.concatenate(blocks, axis=0).T.astype(jnp.float32)
        if j == 0:
            first = fields
        for r in range(tile):
            for v in range(variables):
                for m in range(members):
                    at = ((r * variables + v) * members + m) * levels
                    term = (
                        fields[at : at + levels]
                        * local_refs[j][pl.ds((m * tile + r) * levels, levels), :]
                    )
                    sums[r, v] = sums[r, v] + term if (r, v) in sums else term
    for r in range(tile):
        residual = []
        for v in range(variables):
            rows = pl.ds(v * tile + r, levels, stride=variables * tile)
            increment = sums[r, v] * factor
            inc_ref[rows, :] = increment
            residual.append(weight_ref[rows, :] * (increment - depart_ref[rows, :]))
        for m in range(members):
            total = None
            for v in range(variables):
                at = ((r * variables + v) * members + m) * levels
                term = first[at : at + levels] * residual[v]
                total = term if total is None else total + term
            adj_ref[pl.ds((m * tile + r) * levels, levels), :] = total * factor
            far_ref[pl.ds((m * tile + r) * levels, levels), :] = total * factor
    far_ref[pl.ds(members * tile * levels, levels), :] = jnp.zeros((levels, inc_ref.shape[1]), jnp.float32)


def gradient_rows(members, tile, rates_ref, own_ref, near_ref, far_ref, control_ref, out_ref):
    levels = rates_ref.shape[1]
    odd, low, high = edges()
    low_on, high_on = low.astype(jnp.float32), high.astype(jnp.float32)
    rates = [rates_ref[step] for step in range(NSTEP)]
    for m in range(members):
        own, near, far = (
            [ref[pl.ds((m * tile + r) * levels, levels), :] for r in range(tile)]
            for ref in (own_ref, near_ref, near_ref if far_ref is None else far_ref)
        )
        done = sweeps(with_halo(own, near, far, odd, low, high), rates, low_on, high_on, tile)
        for r in range(tile):
            rows = pl.ds(m * levels * tile + r, levels, stride=tile)
            out_ref[rows, :] = control_ref[rows, :] + done[r]


def end_kernel(members, tile, rates_ref, own_ref, near_ref, control_ref, out_ref, rows_ref, sem):
    _, low, high = edges()

    @pl.when(jnp.logical_not(low & high))
    def _():
        gradient_rows(members, tile, rates_ref, own_ref, near_ref, None, control_ref, rows_ref)
        copy = pltpu.make_async_copy(rows_ref, out_ref, sem)
        copy.start()
        copy.wait()


def inner_kernel(
    members, tile, rates_ref, own_ref, near_ref, far_ref, control_ref, _, out_ref, rows_ref, sem
):
    _, low, high = edges()

    @pl.when(low & high)
    def _():
        gradient_rows(
            members, tile, rates_ref, own_ref, near_ref, far_ref, control_ref, rows_ref
        )
        copy = pltpu.make_async_copy(rows_ref, out_ref, sem)
        copy.start()
        copy.wait()


def near_pairs(doms):
    return [(i, i ^ 1) for i in range(doms)]


def far_pairs(groups, doms):
    pairs = []
    for g in range(groups):
        for d in range(doms):
            if d in (0, doms - 1):
                pairs.append((g * doms + d, (g ^ 1) * doms + d))
            else:
                pairs.append((g * doms + d, g * doms + (d + 1 if d % 2 else d - 1)))
    return pairs


def core_order(groups, doms):
    return [
        [
            g * doms + 2 * chip + core
            for core in range(2)
            for g in GROUPS
            for chip in CHIPS
        ]
    ]


def beside(x, groups, doms):
    near = lax.ppermute(x, "dom", near_pairs(doms))
    far = lax.ppermute(x, ("grp", "dom"), far_pairs(groups, doms))
    return near, far


def small_device(pert_fcst, control, departures, obs_weight, diff_rate, step_counts):
    members, levels, variables = pert_fcst.shape[:3]
    tile, lons = control.shape[2], control.shape[3]
    groups, doms = lax.axis_size("grp"), lax.axis_size("dom")
    factor = 1.0 / math.sqrt(members * groups - 1)
    fields = members * levels * variables * tile
    flat = control.reshape(-1, lons)
    cells = pert_fcst.shape[-1]
    chosen = pl.pallas_call(
        functools.partial(choice_kernel, tile, lons // doms),
        out_shape=pltpu.VMEM((2 * lons // doms, 2 * cells // doms), jnp.bfloat16),
        out_specs=VMEM,
        cost_estimate=pl.CostEstimate(flops=10**10, bytes_accessed=0, transcendentals=0),
    )()
    tiles, rates = pl.pallas_call(
        functools.partial(pack_kernel, doms, tile, groups),
        out_shape=[
            jax.ShapeDtypeStruct((2, groups, doms // 2, lons // doms, fields), jnp.bfloat16),
            pltpu.VMEM((NSTEP, levels, lons), jnp.float32),
        ],
        in_specs=[VMEM, VMEM, ANY, ANY],
        out_specs=[ANY, VMEM],
        scratch_shapes=[
            pltpu.VMEM((2, doms // 2, lons // doms, fields), jnp.bfloat16),
            pltpu.VMEM((1, levels), jnp.float32),
            pltpu.VMEM((1, levels), jnp.int32),
            pltpu.SemaphoreType.DMA((groups + 2,)),
        ],
    )(
        in_vmem(chosen),
        in_vmem(pert_fcst.reshape(members * levels, variables, -1)),
        diff_rate.reshape(1, -1),
        step_counts.reshape(1, -1),
    )
    near, far = beside(flat, groups, doms)
    received = lax.all_to_all(
        tiles.reshape(-1, *tiles.shape[3:]),
        ("grp", "dom"),
        split_axis=0,
        concat_axis=0,
        tiled=True,
        axis_index_groups=core_order(groups, doms),
    )
    tiles = received.reshape(tiles.shape)
    local = pl.pallas_call(
        functools.partial(localize_kernel, members, tile),
        out_shape=pltpu.VMEM(flat.shape, jnp.float32),
        in_specs=[VMEM] * 4,
        out_specs=VMEM,
        cost_estimate=pl.CostEstimate(flops=10**10, bytes_accessed=0, transcendentals=0),
    )(in_vmem(rates), in_vmem(flat), in_vmem(near), in_vmem(far))
    locals_ = [local] + [
        lax.ppermute(local, "grp", [(i, i ^ j) for i in range(groups)]) for j in range(1, groups)
    ]
    increment, adjoint, for_far = pl.pallas_call(
        functools.partial(adjoint_kernel, members, levels, variables, tile, groups, factor),
        out_shape=[
            pltpu.VMEM((levels * variables * tile, lons), jnp.float32),
            pltpu.VMEM(flat.shape, jnp.float32),
            pltpu.VMEM((flat.shape[0] + levels, lons), jnp.float32),
        ],
        in_specs=[VMEM] * (groups + 3),
        out_specs=[VMEM, VMEM, VMEM],
    )(
        in_vmem(tiles),
        *[in_vmem(x) for x in locals_],
        in_vmem(obs_weight.reshape(-1, lons)),
        in_vmem(departures.reshape(-1, lons)),
    )
    near = lax.ppermute(adjoint, "dom", near_pairs(doms))
    far = lax.ppermute(for_far, ("grp", "dom"), far_pairs(groups, doms))
    at_ends = pl.pallas_call(
        functools.partial(end_kernel, members, tile),
        out_shape=jax.ShapeDtypeStruct(flat.shape, jnp.float32),
        in_specs=[VMEM] * 4,
        out_specs=ANY,
        scratch_shapes=[pltpu.VMEM(flat.shape, jnp.float32), pltpu.SemaphoreType.DMA],
        cost_estimate=pl.CostEstimate(flops=0, bytes_accessed=0, transcendentals=0),
    )(in_vmem(rates), in_vmem(adjoint), in_vmem(near), in_vmem(flat))
    gradient = pl.pallas_call(
        functools.partial(inner_kernel, members, tile),
        out_shape=jax.ShapeDtypeStruct(flat.shape, jnp.float32),
        in_specs=[VMEM] * 5 + [ANY],
        out_specs=ANY,
        scratch_shapes=[pltpu.VMEM(flat.shape, jnp.float32), pltpu.SemaphoreType.DMA],
        input_output_aliases={5: 0},
    )(in_vmem(rates), in_vmem(adjoint), in_vmem(near), in_vmem(far), in_vmem(flat), at_ends)
    return increment.reshape(departures.shape), gradient.reshape(control.shape)


def diffuse(field, diff_rate, step_counts):
    count, me = lax.axis_size("dom"), lax.axis_index("dom")
    forward = [(i, i + 1) for i in range(count - 1)]
    backward = [(target, source) for source, target in forward]
    tile = field.shape[2]
    low = lax.ppermute(field[:, :, tile - NSTEP :], "dom", forward)
    high = lax.ppermute(field[:, :, :NSTEP], "dom", backward)
    wide = jnp.concatenate([low, field, high], axis=2)
    row = lax.broadcasted_iota(jnp.int32, (1, 1, wide.shape[2], 1), 2)
    inside = ((row >= NSTEP) | (me > 0)) & ((row < NSTEP + tile) | (me < count - 1))
    for step in range(NSTEP):
        on = (step < step_counts)[None, :, None, None] & inside
        padded = jnp.pad(wide, ((0, 0), (0, 0), (1, 1), (0, 0)))
        laplace = (
            padded[:, :, 2:]
            + padded[:, :, :-2]
            + jnp.roll(wide, 1, axis=3)
            + jnp.roll(wide, -1, axis=3)
            - 4.0 * wide
        )
        wide = jnp.where(on, wide + diff_rate[None, :, None, None] * laplace, wide)
    return wide[:, :, NSTEP : NSTEP + tile]


def any_device(pert_fcst, control, departures, obs_weight, diff_rate, step_counts):
    members, levels, variables = pert_fcst.shape[:3]
    tile, lons = control.shape[2], control.shape[3]
    doms = lax.axis_size("dom")
    factor = 1.0 / math.sqrt(members * lax.axis_size("grp") - 1)
    localized = diffuse(control, diff_rate, step_counts)
    received = lax.all_to_all(
        pert_fcst.reshape(members * levels * variables, doms, -1),
        "dom",
        split_axis=1,
        concat_axis=1,
        tiled=True,
    )
    perturb = (
        received.reshape(-1, doms, tile, lons // doms)
        .transpose(0, 2, 1, 3)
        .reshape(members, levels, variables, tile, lons)
        .astype(jnp.float32)
    )
    increment = lax.psum(jnp.sum(perturb * localized[:, :, None], axis=0), "grp") * factor
    residual = obs_weight * (increment - departures)
    adjoint = jnp.sum(perturb * residual[None], axis=2) * factor
    return increment, control + diffuse(adjoint, diff_rate, step_counts)


def per_device(pert_fcst, control, departures, obs_weight, diff_rate, step_counts):
    members, levels, variables = pert_fcst.shape[:3]
    tile, lons = control.shape[2], control.shape[3]
    groups, doms = lax.axis_size("grp"), lax.axis_size("dom")
    small = (
        lons == 128
        and levels == 8
        and tile == NSTEP
        and members * levels * variables * tile == 128
        and doms == 2 * len(CHIPS)
        and lons // doms == 16
        and groups == len(GROUPS)
    )
    run = small_device if small else any_device
    return run(pert_fcst, control, departures, obs_weight, diff_rate, step_counts)


def solution(mesh):
    in_specs = (
        P("grp", None, None, "dom", None),
        P("grp", None, "dom", None),
        P(None, None, "dom", None),
        P(None, None, "dom", None),
        P(),
        P(),
    )
    out_specs = (P(None, None, "dom", None), P("grp", None, "dom", None))
    return jax.shard_map(
        per_device, mesh=mesh, in_specs=in_specs, out_specs=out_specs, check_vma=False
    )
```
